256 devices in a mesh: ctx: 64 (over y_hi, x, z), heads: 4 (over y_lo, core).
Axes of the slice: x: 4, y: 4 (y_hi: 2, y_lo: 2; y = y_hi * 2 + y_lo), z: 8, core: 2. Of those that a mesh axis runs over, the one named last changes fastest.
Arguments:
- queries: bfloat16 [64, 128, 576], P(None, 'heads'), may hold values from -60 to 60
- latents: bfloat16 [65536, 576], P('ctx'), may hold values from -6 to 6
- index_queries: bfloat16 [64, 64, 128], P(None, 'heads'), may hold values from -24 to 24
- index_keys: bfloat16 [65536, 128], P('ctx'), may hold values from -6 to 6
- index_weights: float32 [64, 64], P(None, 'heads'), may hold values from -15 to 15
- positions: int32 [64], replicated, may hold values from 16384 to 65535, as said below
Outputs:
- grad_index_queries: float32 [64, 64, 128], P(None, 'heads')
- grad_index_keys: float32 [65536, 128], P(('ctx', 'heads'))
The draws below stay inside these ranges and needn't reach their ends.
Inputs may be any that keep to these rules, and one draw needn't show every extreme that they name: Row q sees keys 0 to positions[q]. One row sits at 65535 and one at 16384.
All inputs are finite; a program needn't handle non-finite values.
Results may differ from the reference program's by a relative error of at most 0.0028.
Values sent between devices are 32-bit elements; how exact they have to be, the bound alone decides.
A program may use at most 64 MiB of HBM per device.

```python
import jax
import jax.numpy as jnp
from jax import lax

Q = 64
KEY_DEV = 1024
H = 128
LAT = 576
HI = 64
DI = 128
TOKENS = 65536
LOSS_SCALE = 1024


def main_pair(key):
    latent_values = jnp.clip(jax.random.normal(jax.random.fold_in(key, 101), (TOKENS, LAT), jnp.float32), -6.0, 6.0)
    query_values = jnp.clip(jax.random.normal(jax.random.fold_in(key, 102), (Q, H, LAT), jnp.float32), -6.0, 6.0)
    return (latent_values, query_values)


def index_triple(key):
    key_values = jnp.clip(jax.random.normal(jax.random.fold_in(key, 201), (TOKENS, DI), jnp.float32), -6.0, 6.0)
    query_values = jnp.clip(jax.random.normal(jax.random.fold_in(key, 202), (Q, HI, DI), jnp.float32), -6.0, 6.0)
    weight_values = jnp.clip(2.5 * jax.random.normal(jax.random.fold_in(key, 203), (Q, HI), jnp.float32), -15.0, 15.0)
    return (key_values, query_values, weight_values)


def draw_queries(key, part):
    return main_pair(key)[1].astype(jnp.bfloat16)


def draw_latents(key, part):
    return main_pair(key)[0].astype(jnp.bfloat16)


def draw_index_queries(key, part):
    return index_triple(key)[1].astype(jnp.bfloat16)


def draw_index_keys(key, part):
    return index_triple(key)[0].astype(jnp.bfloat16)


def draw_index_weights(key, part):
    return index_triple(key)[2].astype(jnp.float32)


def draw_positions(key, part):
    lowest = TOKENS // 4
    drawn = jax.random.randint(jax.random.fold_in(key, 301), (Q,), lowest, TOKENS)
    order = jax.random.permutation(jax.random.fold_in(key, 302), Q)
    drawn = drawn.at[order[0]].set(TOKENS - 1)
    drawn = drawn.at[order[1]].set(lowest)
    return drawn.astype(jnp.int32)


def setup_inputs(seed: int = 0) -> dict:
    splits = jax.random.split(jax.random.key(seed), 7)
    queries = draw_queries(jax.random.fold_in(splits[6], 71), 0)
    latents = draw_latents(jax.random.fold_in(splits[6], 71), 0)
    index_queries = draw_index_queries(jax.random.fold_in(splits[6], 71), 0)
    index_keys = draw_index_keys(jax.random.fold_in(splits[6], 71), 0)
    index_weights = draw_index_weights(jax.random.fold_in(splits[6], 71), 0)
    positions = draw_positions(jax.random.fold_in(splits[6], 71), 0)
    return dict(queries=queries, latents=latents, index_queries=index_queries, index_keys=index_keys, index_weights=index_weights, positions=positions)


score_scale = 192 ** -0.5
negative_fill = -1e30


def reference(queries, latents, index_queries, index_keys, index_weights, positions):
    nblocks = TOKENS // KEY_DEV
    flat_queries = queries.reshape(Q * H, LAT)
    flat_index = index_queries.reshape(Q * HI, DI)
    latent_blocks = latents.reshape(nblocks, KEY_DEV, LAT)
    key_blocks = index_keys.reshape(nblocks, KEY_DEV, DI)
    starts = jnp.arange(nblocks, dtype=jnp.int32) * KEY_DEV
    index_scale = (HI * DI) ** -0.5
    scaled_weights = index_weights * index_scale

    def block_view(offset):
        key_pos = offset + jnp.arange(KEY_DEV, dtype=jnp.int32)
        return key_pos[None, :] <= positions[:, None]

    def block_scores(latent_block, offset):
        products = jnp.dot(flat_queries, latent_block.T, preferred_element_type=jnp.float32)
        products = products.reshape(Q, H, KEY_DEV) * score_scale
        visible_now = block_view(offset)
        return jnp.where(visible_now[:, None, :], products, negative_fill), visible_now

    def first_step(running, inputs):
        run_max, run_total = running
        scores, visible_now = block_scores(inputs[0], inputs[1])
        new_max = jnp.maximum(run_max, jnp.max(scores, axis=2))
        added = jnp.sum(jnp.where(visible_now[:, None, :], jnp.exp(scores - new_max[:, :, None]), 0.0), axis=2)
        run_total = run_total * jnp.exp(run_max - new_max) + added
        return (new_max, run_total), None

    initial = (jnp.full((Q, H), negative_fill, jnp.float32), jnp.zeros((Q, H), jnp.float32))
    (row_max, row_total), ignored = lax.scan(first_step, initial, (latent_blocks, starts))

    def target_block(inputs):
        scores, visible_now = block_scores(inputs[0], inputs[1])
        weights_now = jnp.where(visible_now[:, None, :], jnp.exp(scores - row_max[:, :, None]) / row_total[:, :, None], 0.0)
        return jnp.sum(weights_now, axis=1)

    target = lax.map(target_block, (latent_blocks, starts))
    target = jnp.transpose(target, (1, 0, 2)).reshape(Q, TOKENS) * (1.0 / H)

    def index_dots(key_block):
        return jnp.dot(flat_index, key_block.T, preferred_element_type=jnp.float32).reshape(Q, HI, KEY_DEV)

    def logit_block(key_block):
        return jnp.sum(scaled_weights[:, :, None] * jnp.maximum(index_dots(key_block), 0.0), axis=1)

    logits = lax.map(logit_block, key_blocks)
    logits = jnp.transpose(logits, (1, 0, 2)).reshape(Q, TOKENS)
    visible_all = jnp.arange(TOKENS, dtype=jnp.int32)[None, :] <= positions[:, None]
    masked = jnp.where(visible_all, logits, negative_fill)
    row_peak = jnp.max(masked, axis=1)
    row_mass = jnp.sum(jnp.where(visible_all, jnp.exp(masked - row_peak[:, None]), 0.0), axis=1)
    index_probs = jnp.where(visible_all, jnp.exp(masked - row_peak[:, None]) / row_mass[:, None], 0.0)
    logit_grad = LOSS_SCALE * (index_probs - target)
    grad_blocks = jnp.transpose(logit_grad.reshape(Q, nblocks, KEY_DEV), (1, 0, 2))

    def back_step(running, inputs):
        key_block, grad_block = inputs
        dots_now = index_dots(key_block)
        coefficient = jnp.where(dots_now > 0.0, grad_block[:, None, :] * scaled_weights[:, :, None], 0.0)
        coefficient = coefficient.astype(jnp.bfloat16).reshape(Q * HI, KEY_DEV)
        running = running + jnp.dot(coefficient, key_block, preferred_element_type=jnp.float32)
        key_grad = lax.dot_general(coefficient, flat_index, (((0,), (0,)), ((), ())), preferred_element_type=jnp.float32)
        return running, key_grad

    grad_queries, grad_keys = lax.scan(back_step, jnp.zeros((Q * HI, DI), jnp.float32), (key_blocks, grad_blocks))
    return grad_queries.reshape(Q, HI, DI), grad_keys.reshape(TOKENS, DI)
```

```python
import functools

import jax
import jax.numpy as jnp
from jax import lax
from jax.experimental import pallas as pl
from jax.experimental.pallas import tpu as pltpu
from jax.sharding import PartitionSpec as P

MESH = pl.DeviceIdType.MESH
F32 = jnp.float32
BF16 = jnp.bfloat16

Q, H, HI, DI = 64, 128, 64, 128
NZ = 8
NG = 8
HL = 32
JL = 16
KEYS = 1024
QB = 8
NB = Q // QB
LOG2E = 1.4426950408889634
SCORE_SCALE = (192 ** (-0.5)) * LOG2E
INDEX_SCALE = (HI * DI) ** (-0.5)
FILL = -1e30
LOSS_SCALE = 1024.0


def kernel(
    pos_ref, q_ref, lat_ref, iq_ref, ik_ref, wt_ref,
    gq_ref, gk_ref,
    prod, ex, iqf, iqp, iqt, ikt, dots, wpad, w_ref, coef,
    lg, lg_rc, lg_ry, lg_fin,
    tg, tg_rc, tg_ry, tg_fin,
    st, st_rz, st2, st_rx, fac,
    gq_tmp, gq, gq_rx, gq_s1, gq_rz, blk,
    gk_p, gk_rc, gk_s, gk_ry,
    pair_send, pair_recv, send_z, recv_z, send_x, recv_x,
):
    c = lax.axis_index("ctx")
    h = lax.axis_index("heads")
    z, g = c % NZ, c // NZ
    core, ylo = h % 2, h // 2
    core_peer = (c, ylo * 2 + (1 - core))
    ylo_peer = (c, (1 - ylo) * 2 + core)
    far = (4, 3, 5, 2, 6, 1, 7)
    z_ids = [(z + k) % NZ for k in far]
    g_ids = [(g + k) % NG for k in far]
    z_peers = [(g * NZ + i, h) for i in z_ids]
    g_peers = [(i * NZ + z, h) for i in g_ids]
    peers = z_peers + g_peers + [core_peer, ylo_peer]

    barrier = pltpu.get_barrier_semaphore()
    for p in peers:
        pl.semaphore_signal(barrier, inc=1, device_id=p, device_id_type=MESH)

    def remote(src, dst, send, recv, peer):
        return pltpu.make_async_remote_copy(
            src_ref=src, dst_ref=dst, send_sem=send, recv_sem=recv,
            device_id=peer, device_id_type=MESH,
        )

    def pair(slot, src, dst, peer):
        return remote(src, dst, pair_send.at[slot], pair_recv.at[slot], peer)

    iqf[...] = iq_ref[...].astype(F32)

    def permute(b, _):
        for j in range(0, JL, 2):
            two = [iqf[pl.ds(b * 128 + j + i, QB, stride=JL), :] for i in range(2)]
            iqp[pl.ds(b * 128 + j * QB, 2 * QB), :] = jnp.concatenate(two, axis=0).astype(BF16)
        return 0

    lax.fori_loop(0, NB, permute, 0)
    ikt[...] = ik_ref[...].T
    iqt[...] = iqp[...].T
    wpad[...] = jnp.zeros_like(wpad)
    wpad[0:JL, 0:Q] = wt_ref[...] * INDEX_SCALE
    w_ref[...] = wpad[...].T

    key_pos = c * KEYS + lax.broadcasted_iota(jnp.int32, (QB, KEYS), 1)
    row_iota = lax.broadcasted_iota(jnp.int32, (QB, 1), 0)
    lane = lax.broadcasted_iota(jnp.int32, (QB, 128), 1)

    def visible_of(b):
        col = jnp.zeros((QB, 1), jnp.int32)
        for i in range(QB):
            col = jnp.where(row_iota == i, pos_ref[b * QB + i], col)
        return key_pos <= col

    def index_block(b, _):
        rows = pl.ds(pl.multiple_of(b * 128, 128), 128)
        dots[rows, :] = jnp.dot(iqp[rows, :], ikt[...], preferred_element_type=F32)
        wb = w_ref[pl.ds(pl.multiple_of(b * QB, QB), QB), :]
        total = jnp.zeros((QB, KEYS), F32)
        for j in range(JL):
            d = dots[pl.ds(pl.multiple_of(b * 128 + j * QB, QB), QB), :]
            total = total + wb[:, j : j + 1] * jnp.maximum(d, 0.0)
        lg[pl.ds(pl.multiple_of(b * QB, QB), QB), :] = jnp.where(visible_of(b), total, FILL)
        return 0

    lax.fori_loop(0, NB, index_block, 0)

    def attention_block(b, _):
        rows = pl.ds(pl.multiple_of(b * (QB * HL), QB * HL), QB * HL)
        for n in range(KEYS // 256):
            part = jnp.dot(
                q_ref[rows, :], lat_ref[:, n * 256 : (n + 1) * 256], preferred_element_type=F32
            )
            prod[2 * n] = part[:, :128]
            prod[2 * n + 1] = part[:, 128:]
        vis = visible_of(b)
        first = HL * (b % 4)
        group = pl.ds(pl.multiple_of(QB * (b // 4), QB), QB)
        group2 = pl.ds(pl.multiple_of(16 + QB * (b // 4), QB), QB)

        def head(k, carry):
            ms, ls = carry
            x = jnp.concatenate(
                [prod[n, pl.ds(k, QB, stride=HL), :] for n in range(KEYS // 128)], axis=1
            )
            x = jnp.where(vis, x * SCORE_SCALE, FILL)
            m = jnp.max(x, axis=1, keepdims=True)
            e = jnp.exp2(x - m)
            l = jnp.sum(e, axis=1, keepdims=True)
            ex[pl.ds(pl.multiple_of(b * (QB * HL) + k * QB, QB), QB), :] = e
            here = lane == first + k
            return jnp.where(here, m, ms), jnp.where(here, l, ls)

        ms, ls = lax.fori_loop(0, HL, head, (st[group, :], st[group2, :]), unroll=True)
        st[group, :] = ms
        st[group2, :] = ls
        return 0

    st[...] = jnp.zeros_like(st)
    half = pl.ds(pl.multiple_of(core * 32, 32), 32)
    other = pl.ds(pl.multiple_of((1 - core) * 32, 32), 32)

    lax.fori_loop(0, 2, attention_block, 0)
    pl.semaphore_wait(barrier, len(peers))
    c1 = pair(0, lg.at[other], lg_rc, core_peer)
    c1.start()
    lax.fori_loop(2, 4, attention_block, 0)
    c1.wait()
    lg[half, :] = lg[half, :] + lg_rc[...]
    c2 = pair(1, lg.at[half], lg_ry, ylo_peer)
    c2.start()
    lax.fori_loop(4, 7, attention_block, 0)
    c2.wait()
    lg_fin[half, :] = lg[half, :] + lg_ry[...]
    c3 = pair(2, lg_fin.at[half], lg_fin.at[half], core_peer)
    c3.start()
    lax.fori_loop(7, 8, attention_block, 0)
    c3.wait()

    def index_stats(b, ix):
        x = lg_fin[pl.ds(pl.multiple_of(b * QB, QB), QB), :] * LOG2E
        m = jnp.max(x, axis=1, keepdims=True)
        l = jnp.sum(jnp.exp2(x - m), axis=1, keepdims=True)
        return jnp.where(lane == b, m, jnp.where(lane == b + 64, l, ix))

    st[32:40, :] = lax.fori_loop(0, NB, index_stats, jnp.zeros((QB, 128), F32))

    def exchange(src, dst, sends, recvs, targets):
        copies = [remote(src, dst.at[k], sends.at[k], recvs.at[k], p) for k, p in enumerate(targets)]
        for copy in copies:
            copy.start()
        for copy in copies:
            copy.wait()

    def combine(own, received):
        parts = [own[...]] + [received[k] for k in range(7)]
        top = functools.reduce(jnp.maximum, [p[0:16] for p in parts])
        mass = sum(p[16:32] * jnp.exp2(p[0:16] - top) for p in parts)
        peak = functools.reduce(jnp.maximum, [p[32:40] for p in parts])
        low = lane < 64
        imass = sum(
            p[32:40] * pltpu.roll(jnp.exp2(jnp.where(low, p[32:40] - peak, 0.0)), 64, 1)
            for p in parts
        )
        return top, mass, jnp.where(low, peak, imass)

    exchange(st, st_rz, send_z.at[0], recv_z.at[0], z_peers)
    top, mass, idx = combine(st, st_rz)
    st2[0:16, :] = top
    st2[16:32, :] = mass
    st2[32:40, :] = idx
    exchange(st2, st_rx, send_x.at[0], recv_x.at[0], g_peers)
    top, mass, idx = combine(st2, st_rx)
    fac[0:16, :] = jnp.exp2(st[0:16, :] - top) / mass
    fac[16:24, :] = idx

    def target_block(b, _):
        f = fac[pl.ds(pl.multiple_of(QB * (b // 4), QB), QB), :]
        f = pltpu.roll(f, (128 - HL * (b % 4)) % 128, 1)
        total = jnp.zeros((QB, KEYS), F32)
        for k in range(HL):
            e = ex[pl.ds(pl.multiple_of(b * (QB * HL) + k * QB, QB), QB), :]
            total = total + e * f[:, k : k + 1]
        tg[pl.ds(pl.multiple_of(b * QB, QB), QB), :] = total
        return 0

    lax.fori_loop(0, NB, target_block, 0)
    c4 = pair(3, tg.at[other], tg_rc, core_peer)
    c4.start()
    c4.wait()
    tg[half, :] = tg[half, :] + tg_rc[...]
    c5 = pair(4, tg.at[half], tg_ry, ylo_peer)
    c5.start()
    c5.wait()
    tg_fin[half, :] = tg[half, :] + tg_ry[...]
    c6 = pair(5, tg_fin.at[half], tg_fin.at[half], core_peer)
    c6.start()
    c6.wait()

    def grad_block(b):
        rows = pl.ds(pl.multiple_of(b * QB, QB), QB)
        ix = fac[16:24, :]
        peak = jnp.sum(jnp.where(lane == b, ix, 0.0), axis=1, keepdims=True)
        mass = jnp.sum(jnp.where(lane == b + 64, ix, 0.0), axis=1, keepdims=True)
        probs = jnp.exp2(lg_fin[rows, :] * LOG2E - peak) * (1.0 / mass)
        grad = LOSS_SCALE * (probs - tg_fin[rows, :] * (1.0 / H))
        wb = w_ref[rows, :]
        for j in range(0, JL, 2):
            two = []
            for i in (j, j + 1):
                d = dots[pl.ds(pl.multiple_of(b * 128 + i * QB, QB), QB), :]
                two.append(jnp.where(d > 0.0, grad * wb[:, i : i + 1], 0.0))
            at = pl.ds(pl.multiple_of(b * 128 + j * QB, 2 * QB), 2 * QB)
            coef[at, :] = jnp.concatenate(two, axis=0).astype(BF16)
        here = pl.ds(pl.multiple_of(b * 128, 128), 128)
        gq_tmp[...] = jnp.dot(coef[here, :], ik_ref[...], preferred_element_type=F32)
        for i in range(QB):
            gq[b, pl.ds(i * JL, JL), :] = gq_tmp[pl.ds(i, JL, stride=QB), :]

    def grad_send(k, _):
        b = (g + 1 + k) % NG
        grad_block(b)
        remote(
            gq.at[b], gq_rx.at[k], send_x.at[1, k], recv_x.at[1, k], (b * NZ + z, h)
        ).start()
        return 0

    lax.fori_loop(0, 7, grad_send, 0)
    grad_block(g)

    for piece in range(4):
        gk_p[piece % 2, piece // 2] = jnp.dot(
            iqt[...], coef[:, piece * 256 : (piece + 1) * 256], preferred_element_type=F32
        )
    c7 = pair(6, gk_p.at[1 - core], gk_rc, core_peer)
    c7.start()
    c7.wait()
    gk_s[...] = gk_p[core] + gk_rc[...]
    c8 = pair(7, gk_s.at[1 - ylo], gk_ry, ylo_peer)
    c8.start()

    total = gq[g]
    for k in range(7):
        copy = remote(
            gq.at[(g + 1 + k) % NG], gq_rx.at[k], send_x.at[1, k], recv_x.at[1, k],
            (((g + 1 + k) % NG) * NZ + z, h),
        )
        copy.wait()
        total = total + gq_rx[k]
    gq_s1[...] = total.reshape(NZ, JL, DI)
    copies = [
        remote(gq_s1.at[i], gq_rz.at[k], send_z.at[1, k], recv_z.at[1, k], p)
        for k, (i, p) in enumerate(zip(z_ids, z_peers))
    ]
    for copy in copies:
        copy.start()
    for copy in copies:
        copy.wait()
    total = gq_s1[z]
    for k in range(7):
        total = total + gq_rz[k]
    blk[z] = total
    copies = [
        remote(blk.at[z], blk.at[z], send_z.at[2, k], recv_z.at[2, k], p)
        for k, p in enumerate(z_peers)
    ]
    for copy in copies:
        copy.start()
    c8.wait()
    gk_ref[...] = (gk_s[ylo] + gk_ry[...]).T
    for copy in copies:
        copy.wait()
    mine = gq_ref.at[pl.ds(pl.multiple_of(g * 128, 128), 128)]
    gq_ref[pl.ds(pl.multiple_of(g * 128, 128), 128), :] = blk[...].reshape(128, DI)
    copies = [
        remote(mine, mine, send_x.at[2, k], recv_x.at[2, k], p) for k, p in enumerate(g_peers)
    ]
    for copy in copies:
        copy.start()
    for copy in copies:
        copy.wait()


def body(queries, latents, index_queries, index_keys, index_weights, positions):
    vmem = pl.BlockSpec(memory_space=pltpu.VMEM)
    smem = pl.BlockSpec(memory_space=pltpu.SMEM)
    rows = Q * HL
    v = pltpu.VMEM
    dma = pltpu.SemaphoreType.DMA
    scratch = [
        v((KEYS // 128, QB * HL, 128), F32),
        v((rows, KEYS), F32),
        v((Q * JL, DI), F32),
        v((Q * JL, DI), BF16),
        v((DI, Q * JL), BF16),
        v((DI, KEYS), BF16),
        v((Q * JL, KEYS), F32),
        v((128, 128), F32),
        v((128, 128), F32),
        v((Q * JL, KEYS), BF16),
    ]
    for _ in range(2):
        scratch += [v((Q, KEYS), F32), v((32, KEYS), F32), v((32, KEYS), F32), v((Q, KEYS), F32)]
    scratch += [
        v((40, 128), F32), v((7, 40, 128), F32), v((40, 128), F32), v((7, 40, 128), F32),
        v((24, 128), F32),
        v((128, DI), F32), v((NB, 128, DI), F32), v((7, 128, DI), F32), v((NZ, JL, DI), F32),
        v((7, JL, DI), F32), v((NZ, JL, DI), F32),
        v((2, 2, DI, 256), F32), v((2, DI, 256), F32), v((2, DI, 256), F32), v((DI, 256), F32),
        dma((8,)), dma((8,)), dma((3, 7)), dma((3, 7)), dma((3, 7)), dma((3, 7)),
    ]
    grad_queries, grad_keys = pl.pallas_call(
        kernel,
        out_shape=(
            jax.ShapeDtypeStruct((Q * JL, DI), F32),
            jax.ShapeDtypeStruct((KEYS // 4, DI), F32),
        ),
        in_specs=[smem] + [vmem] * 5,
        out_specs=(vmem, vmem),
        scratch_shapes=scratch,
        compiler_params=pltpu.CompilerParams(
            collective_id=0, has_side_effects=True, vmem_limit_bytes=48 * 1024 * 1024
        ),
    )(
        positions,
        queries.reshape(rows, queries.shape[2]),
        latents.T,
        index_queries.reshape(Q * JL, DI),
        index_keys,
        index_weights.T,
    )
    return grad_queries.reshape(Q, JL, DI), grad_keys


def solution(mesh):
    placed = (
        P(None, "heads", None),
        P("ctx", None),
        P(None, "heads", None),
        P("ctx", None),
        P(None, "heads"),
        P(),
    )
    return jax.shard_map(
        body,
        mesh=mesh,
        in_specs=placed,
        out_specs=(P(None, "heads", None), P(("ctx", "heads"), None)),
        check_vma=False,
    )
```

```python
import functools

import jax
import jax.numpy as jnp
from jax import lax
from jax.experimental import pallas as pl
from jax.experimental.pallas import tpu as pltpu
from jax.sharding import PartitionSpec as P

MESH = pl.DeviceIdType.MESH
F32 = jnp.float32
BF16 = jnp.bfloat16

Q, H, HI, DI = 64, 128, 64, 128
NZ = 8
NG = 8
HL = 32
JL = 16
KEYS = 1024
QB = 8
NB = Q // QB
CH = 32
LOG2E = 1.4426950408889634
SCORE_SCALE = (192 ** (-0.5)) * LOG2E
INDEX_SCALE = (HI * DI) ** (-0.5)
FILL = -1e30
LOSS_SCALE = 1024.0


def kernel(
    pos_ref, q_hbm, lat_hbm, iq_hbm, ik_hbm, wt_hbm,
    gq_ref, gk_ref,
    q_ref, lat_ref, iq_ref, ik_ref, wt_ref,
    prod_a, prod_b, mb, ex, iqf, iqp, iqt, ikt, dots, wpad, w_ref, coef,
    lg, lg_rc, lg_ry, lg_fin,
    tg, tg_rc, tg_ry, tg_fin,
    st, st_rz, st2, st_rx, fac,
    gq_tmp, gq, gq_rx, gz, gz_rx,
    gk_p, gk_rc, gk_s, gk_ry,
    load_sem, pair_send, pair_recv, send_z, recv_z, send_x, recv_x,
):
    c = lax.axis_index("ctx")
    h = lax.axis_index("heads")
    z, g = c % NZ, c // NZ
    core, ylo = h % 2, h // 2
    core_peer = (c, ylo * 2 + (1 - core))
    ylo_peer = (c, (1 - ylo) * 2 + core)
    far = (4, 3, 5, 2, 6, 1, 7)
    z_ids = [(z + k) % NZ for k in far]
    g_ids = [(g + k) % NG for k in far]
    z_peers = [(g * NZ + i, h) for i in z_ids]
    g_peers = [(i * NZ + z, h) for i in g_ids]
    peers = z_peers + g_peers + [core_peer, ylo_peer]

    def load(k, src, dst):
        copy = pltpu.make_async_copy(src, dst, load_sem.at[k])
        copy.start()
        return copy

    first_rows, last_rows = pl.ds(0, CH * HL), pl.ds(CH * HL, CH * HL)
    l_iq = load(0, iq_hbm, iq_ref)
    l_ik = load(1, ik_hbm, ik_ref)
    l_wt = load(2, wt_hbm, wt_ref)
    l_lat = load(3, lat_hbm, lat_ref)
    l_q0 = load(4, q_hbm.at[first_rows], q_ref.at[first_rows])
    l_q1 = load(5, q_hbm.at[last_rows], q_ref.at[last_rows])

    barrier = pltpu.get_barrier_semaphore()
    for p in peers:
        pl.semaphore_signal(barrier, inc=1, device_id=p, device_id_type=MESH)

    def remote(src, dst, send, recv, peer):
        return pltpu.make_async_remote_copy(
            src_ref=src, dst_ref=dst, send_sem=send, recv_sem=recv,
            device_id=peer, device_id_type=MESH,
        )

    def pair(slot, src, dst, peer):
        copy = remote(src, dst, pair_send.at[slot], pair_recv.at[slot], peer)
        copy.start()
        return copy

    def spread(slot, sends, recvs, targets, src, dst):
        copies = [
            remote(src(k), dst(k), sends.at[slot, k], recvs.at[slot, k], p)
            for k, p in enumerate(targets)
        ]
        for copy in copies:
            copy.start()
        return copies

    def wait(copies):
        for copy in copies:
            copy.wait()

    lane = lax.broadcasted_iota(jnp.int32, (QB, 128), 1)
    sub = lax.broadcasted_iota(jnp.int32, (QB, 128), 0)
    key_pos = c * KEYS + lane
    row_iota = lax.broadcasted_iota(jnp.int32, (QB, 1), 0)
    GROUPS = KEYS // 128

    def lanes(n):
        return slice(n * 128, (n + 1) * 128)

    def aligned(start, size, by=None):
        return pl.ds(pl.multiple_of(start, by or size), size)

    def tree(op, parts):
        parts = list(parts)
        while len(parts) > 1:
            parts = [op(*parts[i : i + 2]) if i + 1 < len(parts) else parts[i] for i in range(0, len(parts), 2)]
        return parts[0]

    l_iq.wait()
    iqf[...] = iq_ref[...].astype(F32)

    def permute(b, _):
        for j in range(0, JL, 2):
            two = [iqf[pl.ds(b * 128 + j + i, QB, stride=JL), :] for i in range(2)]
            iqp[aligned(b * 128 + j * QB, 2 * QB), :] = jnp.concatenate(two, axis=0).astype(BF16)
        return 0

    lax.fori_loop(0, NB, permute, 0)
    iqt[...] = iqp[...].T
    l_ik.wait()
    ikt[...] = ik_ref[...].T
    l_wt.wait()
    wpad[...] = jnp.zeros_like(wpad)
    wpad[0:JL, 0:Q] = wt_ref[...] * INDEX_SCALE
    w_ref[...] = wpad[...].T

    def index_block(b, _):
        rows = aligned(b * 128, 128)
        dots[rows, :] = jnp.dot(iqp[rows, :], ikt[...], preferred_element_type=F32)
        wb = w_ref[aligned(b * QB, QB), :]
        ws = [jnp.broadcast_to(wb[:, j : j + 1], (QB, 128)) for j in range(JL)]
        col = jnp.zeros((QB, 1), jnp.int32)
        for i in range(QB):
            col = jnp.where(row_iota == i, pos_ref[b * QB + i], col)
        col = jnp.broadcast_to(col, (QB, 128))
        for n in range(GROUPS):
            total = tree(jnp.add, [
                ws[j] * jnp.maximum(dots[aligned(b * 128 + j * QB, QB), lanes(n)], 0.0)
                for j in range(JL)
            ])
            lg[aligned(b * QB, QB), lanes(n)] = jnp.where(key_pos + n * 128 <= col, total, FILL)
        return 0

    lax.fori_loop(0, NB, index_block, 0)

    def multiply(b, prod):
        rows = aligned(b * (QB * HL), QB * HL)
        for n in range(KEYS // 256):
            at = slice(n * 256, (n + 1) * 256)
            prod[:, at] = jnp.dot(q_ref[rows, :], lat_ref[:, at], preferred_element_type=F32)

    def softmax(b, prod, carry):
        local = b % (CH // QB) * QB

        def peaks(k, ms):
            pos = pos_ref[b * QB + k]
            vis = [key_pos + n * 128 <= pos for n in range(GROUPS)]
            for i in range(HL // QB):
                rows = aligned(k * HL + i * QB, QB)
                m = tree(jnp.maximum, [
                    jnp.where(vis[n], prod[rows, lanes(n)], FILL) for n in range(GROUPS)
                ])
                m = jnp.broadcast_to(jnp.max(m, axis=1, keepdims=True) * SCORE_SCALE, (QB, 128))
                mb[rows, :] = m
                ms = jnp.where(lane == i * 32 + local + k, m, ms)
            return ms

        def masses(k, ls):
            pos = pos_ref[b * QB + k]
            vis = [key_pos + n * 128 <= pos for n in range(GROUPS)]
            for i in range(HL // QB):
                rows = aligned(k * HL + i * QB, QB)
                m = mb[rows, :]
                to = aligned(b * (QB * HL) + k * HL + i * QB, QB)
                es = []
                for n in range(GROUPS):
                    e = jnp.exp2(prod[rows, lanes(n)] * SCORE_SCALE - m)
                    e = jnp.where(vis[n], e, 0.0)
                    ex[to, lanes(n)] = e
                    es.append(e)
                l = jnp.sum(tree(jnp.add, es), axis=1, keepdims=True)
                ls = jnp.where(lane == i * 32 + local + k, l, ls)
            return ls

        ms = lax.fori_loop(0, QB, peaks, carry[0], unroll=True)
        ls = lax.fori_loop(0, QB, masses, carry[1], unroll=True)
        return ms, ls

    def two_blocks(i, carry):
        multiply(2 * i + 1, prod_b)
        carry = softmax(2 * i, prod_a, carry)
        multiply(jnp.minimum(2 * i + 2, NB - 1), prod_a)
        return softmax(2 * i + 1, prod_b, carry)

    def attention(first, last, carry):
        return lax.fori_loop(first, last, two_blocks, carry)

    zero = jnp.zeros((QB, 128), F32)
    half = aligned(core * 32, 32)
    other = aligned((1 - core) * 32, 32)

    l_lat.wait()
    l_q0.wait()
    multiply(0, prod_a)
    l_q1.wait()
    ms, ls = attention(0, 2, (zero, zero))
    st[0, 0:8, :] = ms
    st[0, 8:16, :] = ls
    pl.semaphore_wait(barrier, len(peers))
    s_z0 = spread(0, send_z, recv_z, z_peers, lambda k: st.at[0, 0:16], lambda k: st_rz.at[0, k, 0:16])
    copy = pair(0, lg.at[other], lg_rc, core_peer)
    carry = attention(2, 3, (zero, zero))
    copy.wait()
    lg[half, :] = lg[half, :] + lg_rc[...]
    copy = pair(1, lg.at[half], lg_ry, ylo_peer)
    ms, ls = attention(3, 4, carry)
    st[1, 0:8, :] = ms
    st[1, 8:16, :] = ls
    copy.wait()
    lg_fin[half, :] = lg[half, :] + lg_ry[...]
    copy = pair(2, lg_fin.at[half], lg_fin.at[half], core_peer)
    copy.wait()

    def index_stats(b, ix):
        rows = aligned(b * QB, QB)
        xs = [lg_fin[rows, lanes(n)] * LOG2E for n in range(GROUPS)]
        m = jnp.max(tree(jnp.maximum, xs), axis=1, keepdims=True)
        mm = jnp.broadcast_to(m, (QB, 128))
        l = jnp.sum(tree(jnp.add, [jnp.exp2(x - mm) for x in xs]), axis=1, keepdims=True)
        return jnp.where(lane == b, m, jnp.where(lane == b + 64, l, ix))

    st[1, 16:24, :] = lax.fori_loop(0, NB, index_stats, zero, unroll=True)
    s_z1 = spread(1, send_z, recv_z, z_peers, lambda k: st.at[1], lambda k: st_rz.at[1, k])

    def combine(own, received, with_index):
        parts = [own[...]] + [received[k] for k in range(7)]
        top = tree(jnp.maximum, [p[0:8] for p in parts])
        mass = tree(jnp.add, [p[8:16] * jnp.exp2(p[0:8] - top) for p in parts])
        if not with_index:
            return top, mass, None
        peak = tree(jnp.maximum, [p[16:24] for p in parts])
        low = lane < 64
        imass = tree(jnp.add, [
            p[16:24] * pltpu.roll(jnp.exp2(jnp.where(low, p[16:24] - peak, 0.0)), 64, 1)
            for p in parts
        ])
        return top, mass, jnp.where(low, peak, imass)

    def combined_z(t):
        top, mass, idx = combine(st.at[t], st_rz.at[t], t == 1)
        st2[t, 0:8, :] = top
        st2[t, 8:16, :] = mass
        if t == 0:
            return spread(
                t, send_x, recv_x, g_peers, lambda k: st2.at[0, 0:16], lambda k: st_rx.at[0, k, 0:16]
            )
        st2[t, 16:24, :] = idx
        return spread(t, send_x, recv_x, g_peers, lambda k: st2.at[1], lambda k: st_rx.at[1, k])

    def factors(t):
        top, mass, idx = combine(st2.at[t], st_rx.at[t], t == 1)
        fac[t] = jnp.exp2(st[t, 0:8, :] - top) / mass
        if t == 1:
            fac[2] = idx

    def turn(x, shift):
        return pltpu.roll(x, shift % QB, 0)

    def gathered(r):
        r = [r[i] for i in (3, 2, 1, 0, 7, 6, 5, 4)]
        low = sub < 4
        a = [
            jnp.where(low, r[i], r[i + 4]) + turn(jnp.where(low, r[i + 4], r[i]), 4)
            for i in range(4)
        ]
        low = sub % 4 < 2
        b = [jnp.where(low, a[i + 2] + turn(a[i + 2], -2), a[i] + turn(a[i], 2)) for i in range(2)]
        return jnp.where(sub % 2 < 1, b[1] + turn(b[1], -1), b[0] + turn(b[0], 1))

    def target(t):
        def block(b, _):
            f = pltpu.roll(fac[t], (128 - QB * b) % 128, 1)
            fs = [
                [jnp.broadcast_to(f[:, i * 32 + k : i * 32 + k + 1], (QB, 128)) for i in range(4)]
                for k in range(QB)
            ]
            for n in range(GROUPS):
                r = []
                for k in range(QB):
                    at = (t * (CH // QB) + b) * (QB * HL) + k * HL
                    r.append(tree(jnp.add, [
                        ex[aligned(at + i * QB, QB), lanes(n)] * fs[k][i] for i in range(4)
                    ]))
                tg[t, aligned(b * QB, QB), lanes(n)] = gathered(r)
            return 0

        lax.fori_loop(0, CH // QB, block, 0)

    part = aligned(core * 16, 16)
    other_part = aligned((1 - core) * 16, 16)

    def core_one(t):
        return pair(3 + t, tg.at[t, other_part], tg_rc.at[t], core_peer)

    def across(t):
        tg[t, part, :] = tg[t, part, :] + tg_rc[t]
        return pair(5 + t, tg.at[t, part], tg_ry.at[t], ylo_peer)

    def core_two(t):
        tg_fin[t, part, :] = tg[t, part, :] + tg_ry[t]
        return pair(7 + t, tg_fin.at[t, part], tg_fin.at[t, part], core_peer)

    def grads(t):
        def block(i, _):
            b = t * (CH // QB) + i
            rows = aligned(b * QB, QB)
            ix = fac[2]
            peak = jnp.sum(jnp.where(lane == b, ix, 0.0), axis=1, keepdims=True)
            mass = jnp.sum(jnp.where(lane == b + 64, ix, 0.0), axis=1, keepdims=True)
            peak = jnp.broadcast_to(peak, (QB, 128))
            share = jnp.broadcast_to(LOSS_SCALE / mass, (QB, 128))
            wb = w_ref[rows, :]
            ws = [jnp.broadcast_to(wb[:, j : j + 1], (QB, 128)) for j in range(JL)]
            for n in range(GROUPS):
                probs = jnp.exp2(lg_fin[rows, lanes(n)] * LOG2E - peak) * share
                grad = probs - tg_fin[t, aligned(i * QB, QB), lanes(n)] * (LOSS_SCALE / H)
                for j in range(0, JL, 2):
                    two = []
                    for jj in (j, j + 1):
                        d = dots[aligned(b * 128 + jj * QB, QB), lanes(n)]
                        two.append(jnp.where(d > 0.0, grad * ws[jj], 0.0))
                    at = aligned(b * 128 + j * QB, 2 * QB)
                    coef[at, lanes(n)] = jnp.concatenate(two, axis=0).astype(BF16)
            here = aligned(b * 128, 128)
            gq_tmp[...] = jnp.dot(coef[here, :], ik_ref[...], preferred_element_type=F32)
            for k in range(QB):
                gq[t, aligned(i * 128 + k * JL, JL), :] = gq_tmp[pl.ds(k, JL, stride=QB), :]
            return 0

        lax.fori_loop(0, CH // QB, block, 0)
        return spread(
            2 + t, send_x, recv_x, g_peers,
            lambda k: gq.at[t, aligned(g_ids[k] * 64, 64)], lambda k: gq_rx.at[t, k],
        )

    def sum_x(t):
        mine = gq[t, aligned(g * 64, 64), :]
        gz[t] = tree(jnp.add, [mine] + [gq_rx[t, k] for k in range(7)])
        gz_rx[t, z] = gz[t]
        return spread(
            2 + t, send_z, recv_z, z_peers, lambda k: gz.at[t], lambda k: gz_rx.at[t, z]
        )

    def sum_z(t):
        mine = aligned(t * 512 + g * 64, 64)
        gq_ref[mine, :] = tree(jnp.add, [gz_rx[t, k] for k in range(NZ)])
        return spread(
            4 + t, send_x, recv_x, g_peers, lambda k: gq_ref.at[mine], lambda k: gq_ref.at[mine]
        )

    wait(s_z0)
    s_x0 = combined_z(0)
    wait(s_z1)
    s_x1 = combined_z(1)
    wait(s_x0)
    factors(0)
    target(0)
    one0 = core_one(0)
    one0.wait()
    across0 = across(0)
    wait(s_x1)
    factors(1)
    target(1)
    one1 = core_one(1)
    across0.wait()
    two0 = core_two(0)
    one1.wait()
    across1 = across(1)
    two0.wait()
    rs0 = grads(0)
    across1.wait()
    two1 = core_two(1)
    two1.wait()
    rs1 = grads(1)

    for piece in range(4):
        gk_p[piece % 2, piece // 2] = jnp.dot(
            iqt[...], coef[:, piece * 256 : (piece + 1) * 256], preferred_element_type=F32
        )
    gk1 = pair(9, gk_p.at[1 - core], gk_rc, core_peer)
    wait(rs0)
    sz0 = sum_x(0)
    gk1.wait()
    gk_s[...] = gk_p[core] + gk_rc[...]
    gk2 = pair(10, gk_s.at[1 - ylo], gk_ry, ylo_peer)
    wait(rs1)
    sz1 = sum_x(1)
    gk2.wait()
    gk_ref[...] = (gk_s[ylo] + gk_ry[...]).T
    wait(sz0)
    ag0 = sum_z(0)
    wait(sz1)
    ag1 = sum_z(1)
    wait(ag0)
    wait(ag1)


def body(queries, latents, index_queries, index_keys, index_weights, positions):
    hbm = pl.BlockSpec(memory_space=pltpu.HBM)
    vmem = pl.BlockSpec(memory_space=pltpu.VMEM)
    smem = pl.BlockSpec(memory_space=pltpu.SMEM)
    rows = Q * HL
    v = pltpu.VMEM
    dma = pltpu.SemaphoreType.DMA
    scratch = [
        v((rows, queries.shape[2]), BF16),
        v((queries.shape[2], KEYS), BF16),
        v((Q * JL, DI), BF16),
        v((KEYS, DI), BF16),
        v((JL, Q), F32),
        v((QB * HL, KEYS), F32),
        v((QB * HL, KEYS), F32),
        v((QB * HL, 128), F32),
        v((rows, KEYS), F32),
        v((Q * JL, DI), F32),
        v((Q * JL, DI), BF16),
        v((DI, Q * JL), BF16),
        v((DI, KEYS), BF16),
        v((Q * JL, KEYS), F32),
        v((128, 128), F32),
        v((128, 128), F32),
        v((Q * JL, KEYS), BF16),
        v((Q, KEYS), F32), v((32, KEYS), F32), v((32, KEYS), F32), v((Q, KEYS), F32),
        v((2, CH, KEYS), F32), v((2, 16, KEYS), F32), v((2, 16, KEYS), F32), v((2, CH, KEYS), F32),
        v((2, 24, 128), F32), v((2, 7, 24, 128), F32),
        v((2, 24, 128), F32), v((2, 7, 24, 128), F32),
        v((3, 8, 128), F32),
        v((128, DI), F32), v((2, 512, DI), F32), v((2, 7, 64, DI), F32),
        v((2, 64, DI), F32), v((2, NZ, 64, DI), F32),
        v((2, 2, DI, 256), F32), v((2, DI, 256), F32), v((2, DI, 256), F32), v((DI, 256), F32),
        dma((6,)), dma((11,)), dma((11,)), dma((4, 7)), dma((4, 7)), dma((6, 7)), dma((6, 7)),
    ]
    grad_queries, grad_keys = pl.pallas_call(
        kernel,
        out_shape=(
            jax.ShapeDtypeStruct((Q * JL, DI), F32),
            jax.ShapeDtypeStruct((KEYS // 4, DI), F32),
        ),
        in_specs=[smem] + [hbm] * 5,
        out_specs=(vmem, vmem),
        scratch_shapes=scratch,
        compiler_params=pltpu.CompilerParams(
            collective_id=0, has_side_effects=True, vmem_limit_bytes=48 * 1024 * 1024
        ),
    )(
        positions,
        queries.reshape(rows, queries.shape[2]),
        latents.T,
        index_queries.reshape(Q * JL, DI),
        index_keys,
        index_weights.T,
    )
    return grad_queries.reshape(Q, JL, DI), grad_keys


def solution(mesh):
    placed = (
        P(None, "heads", None),
        P("ctx", None),
        P(None, "heads", None),
        P("ctx", None),
        P(None, "heads"),
        P(),
    )
    return jax.shard_map(
        body,
        mesh=mesh,
        in_specs=placed,
        out_specs=(P(None, "heads", None), P(("ctx", "heads"), None)),
        check_vma=False,
    )
```

```python
import functools

import jax
import jax.numpy as jnp
from jax import lax
from jax.experimental import pallas as pl
from jax.experimental.pallas import tpu as pltpu
from jax.sharding import PartitionSpec as P

MESH = pl.DeviceIdType.MESH
F32 = jnp.float32
BF16 = jnp.bfloat16

Q, H, HI, DI = 64, 128, 64, 128
NZ = 8
NG = 8
HL = 32
JL = 16
KEYS = 1024
QB = 8
NB = Q // QB
CH = 32
LOG2E = 1.4426950408889634
SCORE_SCALE = (192 ** (-0.5)) * LOG2E
INDEX_SCALE = (HI * DI) ** (-0.5)
FILL = -1e30
LOSS_SCALE = 1024.0


def kernel(
    pos_ref, q_hbm, lat_hbm, iq_hbm, ik_hbm, wt_hbm,
    gq_ref, gk_ref,
    q_ref, lat_ref, iq_ref, ik_ref, wt_ref,
    prod_a, prod_b, mb, ex, iqf, iqp, iqt, ikt, dots, wpad, w_ref, coef,
    lg, lg_rc, lg_ry, lg_fin,
    tg, tg_rc, tg_ry, tg_fin,
    st, st_rz, st2, st_rx, ix, ix_rz, ix2, ix_rx, fac,
    gq_tmp, gq, gq_rx, gz, gz_rx,
    gk_p, gk_rc, gk_s, gk_ry, gsum, gk_out,
    load_sem, pair_send, pair_recv, send_z, recv_z, send_x, recv_x,
):
    c = lax.axis_index("ctx")
    h = lax.axis_index("heads")
    z, g = c % NZ, c // NZ
    core, ylo = h % 2, h // 2
    core_peer = (c, ylo * 2 + (1 - core))
    ylo_peer = (c, (1 - ylo) * 2 + core)
    far = (4, 3, 5, 2, 6, 1, 7)
    z_ids = [(z + k) % NZ for k in far]
    g_ids = [(g + k) % NG for k in far]
    z_peers = [(g * NZ + i, h) for i in z_ids]
    g_peers = [(i * NZ + z, h) for i in g_ids]
    peers = z_peers + g_peers + [core_peer, ylo_peer]

    def load(k, src, dst):
        copy = pltpu.make_async_copy(src, dst, load_sem.at[k])
        copy.start()
        return copy

    first_rows, last_rows = pl.ds(0, CH * HL), pl.ds(CH * HL, CH * HL)
    l_iq = load(0, iq_hbm, iq_ref)
    l_ik = load(1, ik_hbm, ik_ref)
    l_wt = load(2, wt_hbm, wt_ref)
    l_lat = load(3, lat_hbm, lat_ref)
    l_q0 = load(4, q_hbm.at[first_rows], q_ref.at[first_rows])
    l_q1 = load(5, q_hbm.at[last_rows], q_ref.at[last_rows])

    barrier = pltpu.get_barrier_semaphore()
    for p in peers:
        pl.semaphore_signal(barrier, inc=1, device_id=p, device_id_type=MESH)

    def remote(src, dst, send, recv, peer):
        return pltpu.make_async_remote_copy(
            src_ref=src, dst_ref=dst, send_sem=send, recv_sem=recv,
            device_id=peer, device_id_type=MESH,
        )

    def pair(slot, src, dst, peer):
        copy = remote(src, dst, pair_send.at[slot], pair_recv.at[slot], peer)
        copy.start()
        return copy

    def spread(slot, sends, recvs, targets, src, dst):
        copies = [
            remote(src(k), dst(k), sends.at[slot, k], recvs.at[slot, k], p)
            for k, p in enumerate(targets)
        ]
        for copy in copies:
            copy.start()
        return copies

    def wait(copies):
        for copy in copies:
            copy.wait()

    lane = lax.broadcasted_iota(jnp.int32, (QB, 128), 1)
    sub = lax.broadcasted_iota(jnp.int32, (QB, 128), 0)
    key_pos = c * KEYS + lane
    row_iota = lax.broadcasted_iota(jnp.int32, (QB, 1), 0)
    GROUPS = KEYS // 128

    def lanes(n):
        return slice(n * 128, (n + 1) * 128)

    def aligned(start, size, by=None):
        return pl.ds(pl.multiple_of(start, by or size), size)

    def tree(op, parts):
        parts = list(parts)
        while len(parts) > 1:
            parts = [op(*parts[i : i + 2]) if i + 1 < len(parts) else parts[i] for i in range(0, len(parts), 2)]
        return parts[0]

    l_iq.wait()
    iqf[...] = iq_ref[...].astype(F32)

    def permute(b, _):
        for j in range(0, JL, 2):
            two = [iqf[pl.ds(b * 128 + j + i, QB, stride=JL), :] for i in range(2)]
            iqp[aligned(b * 128 + j * QB, 2 * QB), :] = jnp.concatenate(two, axis=0).astype(BF16)
        return 0

    lax.fori_loop(0, NB, permute, 0)
    iqt[...] = iqp[...].T
    l_ik.wait()
    ikt[...] = ik_ref[...].T
    l_wt.wait()
    wpad[...] = jnp.zeros_like(wpad)
    wpad[0:JL, 0:Q] = wt_ref[...] * INDEX_SCALE
    w_ref[...] = wpad[...].T

    for n in range(KEYS // 256):
        at = slice(n * 256, (n + 1) * 256)
        dots[:, at] = jnp.dot(iqp[...], ikt[:, at], preferred_element_type=F32)

    def index_block(b, _):
        wb = w_ref[aligned(b * QB, QB), :]
        ws = [jnp.broadcast_to(wb[:, j : j + 1], (QB, 128)) for j in range(JL)]
        col = jnp.zeros((QB, 1), jnp.int32)
        for i in range(QB):
            col = jnp.where(row_iota == i, pos_ref[b * QB + i], col)
        col = jnp.broadcast_to(col, (QB, 128))
        for n in range(GROUPS):
            total = tree(jnp.add, [
                ws[j] * jnp.maximum(dots[aligned(b * 128 + j * QB, QB), lanes(n)], 0.0)
                for j in range(JL)
            ])
            lg[aligned(b * QB, QB), lanes(n)] = jnp.where(key_pos + n * 128 <= col, total, FILL)
        return 0

    lax.fori_loop(0, NB, index_block, 0, unroll=True)

    def multiply(b, prod):
        rows = aligned(b * (QB * HL), QB * HL)
        for n in range(KEYS // 256):
            at = slice(n * 256, (n + 1) * 256)
            prod[:, at] = jnp.dot(q_ref[rows, :], lat_ref[:, at], preferred_element_type=F32)

    def softmax(b, prod, carry):
        local = b % (CH // QB) * QB

        def peaks(k, ms):
            pos = pos_ref[b * QB + k]
            vis = [key_pos + n * 128 <= pos for n in range(GROUPS)]
            for i in range(HL // QB):
                rows = aligned(k * HL + i * QB, QB)
                m = tree(jnp.maximum, [
                    jnp.where(vis[n], prod[rows, lanes(n)], FILL) for n in range(GROUPS)
                ])
                m = jnp.broadcast_to(jnp.max(m, axis=1, keepdims=True) * SCORE_SCALE, (QB, 128))
                mb[rows, :] = m
                ms = jnp.where(lane == i * 32 + local + k, m, ms)
            return ms

        def masses(k, ls):
            pos = pos_ref[b * QB + k]
            vis = [key_pos + n * 128 <= pos for n in range(GROUPS)]
            for i in range(HL // QB):
                rows = aligned(k * HL + i * QB, QB)
                m = mb[rows, :]
                to = aligned(b * (QB * HL) + k * HL + i * QB, QB)
                es = []
                for n in range(GROUPS):
                    e = jnp.exp2(prod[rows, lanes(n)] * SCORE_SCALE - m)
                    e = jnp.where(vis[n], e, 0.0)
                    ex[to, lanes(n)] = e
                    es.append(e)
                l = jnp.sum(tree(jnp.add, es), axis=1, keepdims=True)
                ls = jnp.where(lane == i * 32 + local + k, l, ls)
            return ls

        ms = lax.fori_loop(0, QB, peaks, carry[0], unroll=True)
        ls = lax.fori_loop(0, QB, masses, carry[1], unroll=True)
        return ms, ls

    def two_blocks(i, carry):
        multiply(2 * i + 1, prod_b)
        carry = softmax(2 * i, prod_a, carry)
        multiply(jnp.minimum(2 * i + 2, NB - 1), prod_a)
        return softmax(2 * i + 1, prod_b, carry)

    def attention(first, last, carry):
        return lax.fori_loop(first, last, two_blocks, carry)

    zero = jnp.zeros((QB, 128), F32)
    half = aligned(core * 32, 32)
    other = aligned((1 - core) * 32, 32)

    l_lat.wait()
    l_q0.wait()
    multiply(0, prod_a)
    l_q1.wait()
    ms, ls = attention(0, 2, (zero, zero))
    st[0, 0:8, :] = ms
    st[0, 8:16, :] = ls
    pl.semaphore_wait(barrier, len(peers))
    s_z0 = spread(0, send_z, recv_z, z_peers, lambda k: st.at[0], lambda k: st_rz.at[0, k])
    lg1 = pair(0, lg.at[other], lg_rc, core_peer)
    carry = attention(2, 3, (zero, zero))
    lg1.wait()
    lg[half, :] = lg[half, :] + lg_rc[...]
    lg2 = pair(1, lg.at[half], lg_ry, ylo_peer)
    ms, ls = attention(3, 4, carry)
    st[1, 0:8, :] = ms
    st[1, 8:16, :] = ls
    s_z1 = spread(1, send_z, recv_z, z_peers, lambda k: st.at[1], lambda k: st_rz.at[1, k])

    def index_stats(b, so_far):
        rows = aligned(b * QB, QB)
        xs = [lg_fin[rows, lanes(n)] * LOG2E for n in range(GROUPS)]
        m = jnp.max(tree(jnp.maximum, xs), axis=1, keepdims=True)
        mm = jnp.broadcast_to(m, (QB, 128))
        l = jnp.sum(tree(jnp.add, [jnp.exp2(x - mm) for x in xs]), axis=1, keepdims=True)
        return jnp.where(lane == b, m, jnp.where(lane == b + 64, l, so_far))

    def combine(own, received):
        parts = [own[...]] + [received[k] for k in range(7)]
        top = tree(jnp.maximum, [p[0:8] for p in parts])
        mass = tree(jnp.add, [p[8:16] * jnp.exp2(p[0:8] - top) for p in parts])
        return top, mass

    def combine_index(own, received):
        parts = [own[...]] + [received[k] for k in range(7)]
        peak = tree(jnp.maximum, parts)
        low = lane < 64
        mass = tree(jnp.add, [
            p * pltpu.roll(jnp.exp2(jnp.where(low, p - peak, 0.0)), 64, 1) for p in parts
        ])
        return jnp.where(low, peak, mass)

    def combined_z(t):
        top, mass = combine(st.at[t], st_rz.at[t])
        st2[t, 0:8, :] = top
        st2[t, 8:16, :] = mass
        return spread(t, send_x, recv_x, g_peers, lambda k: st2.at[t], lambda k: st_rx.at[t, k])

    def factors(t):
        top, mass = combine(st2.at[t], st_rx.at[t])
        fac[t] = jnp.exp2(st[t, 0:8, :] - top) / mass

    def turn(x, shift):
        return pltpu.roll(x, shift % QB, 0)

    def gathered(r):
        r = [r[i] for i in (3, 2, 1, 0, 7, 6, 5, 4)]
        low = sub < 4
        a = [
            jnp.where(low, r[i], r[i + 4]) + turn(jnp.where(low, r[i + 4], r[i]), 4)
            for i in range(4)
        ]
        low = sub % 4 < 2
        b = [jnp.where(low, a[i + 2] + turn(a[i + 2], -2), a[i] + turn(a[i], 2)) for i in range(2)]
        return jnp.where(sub % 2 < 1, b[1] + turn(b[1], -1), b[0] + turn(b[0], 1))

    def target(t):
        f = fac[t]
        for b in range(CH // QB):
            fs = [
                [
                    jnp.broadcast_to(f[:, i * 32 + b * QB + k : i * 32 + b * QB + k + 1], (QB, 128))
                    for i in range(4)
                ]
                for k in range(QB)
            ]
            for n in range(GROUPS):
                r = []
                for k in range(QB):
                    at = (t * (CH // QB) + b) * (QB * HL) + k * HL
                    r.append(tree(jnp.add, [
                        ex[at + i * QB : at + (i + 1) * QB, lanes(n)] * fs[k][i] for i in range(4)
                    ]))
                tg[t, b * QB : (b + 1) * QB, lanes(n)] = gathered(r)

    part = aligned(core * 16, 16)
    other_part = aligned((1 - core) * 16, 16)

    def core_one(t):
        return pair(3 + t, tg.at[t, other_part], tg_rc.at[t], core_peer)

    def across(t):
        tg[t, part, :] = tg[t, part, :] + tg_rc[t]
        return pair(5 + t, tg.at[t, part], tg_ry.at[t], ylo_peer)

    def core_two(t):
        tg_fin[t, part, :] = tg[t, part, :] + tg_ry[t]
        return pair(7 + t, tg_fin.at[t, part], tg_fin.at[t, part], core_peer)

    def grads(t):
        totals = fac[2]
        for i in range(CH // QB):
            b = t * (CH // QB) + i
            rows = slice(b * QB, (b + 1) * QB)
            peak = jnp.broadcast_to(totals[:, b : b + 1], (QB, 128))
            share = jnp.broadcast_to(LOSS_SCALE / totals[:, b + 64 : b + 65], (QB, 128))
            wb = w_ref[rows, :]
            ws = [jnp.broadcast_to(wb[:, j : j + 1], (QB, 128)) for j in range(JL)]
            for n in range(GROUPS):
                probs = jnp.exp2(lg_fin[rows, lanes(n)] * LOG2E - peak) * share
                grad = probs - tg_fin[t, i * QB : (i + 1) * QB, lanes(n)] * (LOSS_SCALE / H)
                for j in range(0, JL, 2):
                    two = []
                    for jj in (j, j + 1):
                        d = dots[b * 128 + jj * QB : b * 128 + (jj + 1) * QB, lanes(n)]
                        two.append(jnp.where(d > 0.0, grad * ws[jj], 0.0))
                    at = slice(b * 128 + j * QB, b * 128 + (j + 2) * QB)
                    coef[at, lanes(n)] = jnp.concatenate(two, axis=0).astype(BF16)
        gq_tmp[...] = jnp.dot(
            coef[t * 512 : (t + 1) * 512, :], ik_ref[...], preferred_element_type=F32
        )
        for i in range(CH // QB):
            for k in range(QB):
                gq[t, i * 128 + k * JL : i * 128 + (k + 1) * JL, :] = gq_tmp[
                    pl.ds(i * 128 + k, JL, stride=QB), :
                ]
        return spread(
            2 + t, send_x, recv_x, g_peers,
            lambda k: gq.at[t, aligned(g_ids[k] * 64, 64)], lambda k: gq_rx.at[t, k],
        )

    def sum_x(t):
        mine = gq[t, aligned(g * 64, 64), :]
        gz[t] = tree(jnp.add, [mine] + [gq_rx[t, k] for k in range(7)])
        gz_rx[t, z] = gz[t]
        return spread(
            2 + t, send_z, recv_z, z_peers, lambda k: gz.at[t], lambda k: gz_rx.at[t, z]
        )

    def sum_z(t):
        mine = aligned(t * 512 + g * 64, 64)
        gsum[t] = tree(jnp.add, [gz_rx[t, k] for k in range(NZ)])
        copies = spread(
            4 + t, send_x, recv_x, g_peers, lambda k: gsum.at[t], lambda k: gq_ref.at[mine]
        )
        return copies + [load(t, gsum.at[t], gq_ref.at[mine])]

    wait(s_z0)
    s_x0 = combined_z(0)
    lg2.wait()
    lg_fin[half, :] = lg[half, :] + lg_ry[...]
    lg3 = pair(2, lg_fin.at[half], lg_fin.at[half], core_peer)
    lg3.wait()
    ix[...] = lax.fori_loop(0, NB, index_stats, zero, unroll=True)
    i_z = spread(4, send_z, recv_z, z_peers, lambda k: ix, lambda k: ix_rz.at[k])
    wait(s_z1)
    s_x1 = combined_z(1)
    wait(s_x0)
    factors(0)
    target(0)
    one0 = core_one(0)
    wait(i_z)
    ix2[...] = combine_index(ix, ix_rz)
    i_x = spread(6, send_x, recv_x, g_peers, lambda k: ix2, lambda k: ix_rx.at[k])
    one0.wait()
    across0 = across(0)
    wait(s_x1)
    factors(1)
    target(1)
    one1 = core_one(1)
    across0.wait()
    two0 = core_two(0)
    one1.wait()
    across1 = across(1)
    wait(i_x)
    fac[2] = combine_index(ix2, ix_rx)
    two0.wait()
    rs0 = grads(0)
    across1.wait()
    two1 = core_two(1)
    two1.wait()
    rs1 = grads(1)

    for piece in range(4):
        gk_p[piece % 2, piece // 2] = jnp.dot(
            iqt[...], coef[:, piece * 256 : (piece + 1) * 256], preferred_element_type=F32
        )
    gk1 = pair(9, gk_p.at[1 - core], gk_rc, core_peer)
    wait(rs0)
    sz0 = sum_x(0)
    gk1.wait()
    gk_s[...] = gk_p[core] + gk_rc[...]
    gk2 = pair(10, gk_s.at[1 - ylo], gk_ry, ylo_peer)
    wait(rs1)
    sz1 = sum_x(1)
    gk2.wait()
    gk_out[...] = (gk_s[ylo] + gk_ry[...]).T
    gk_store = load(2, gk_out, gk_ref)
    wait(sz0)
    ag0 = sum_z(0)
    wait(sz1)
    ag1 = sum_z(1)
    wait(ag0)
    wait(ag1)
    gk_store.wait()


def body(queries, latents, index_queries, index_keys, index_weights, positions):
    hbm = pl.BlockSpec(memory_space=pltpu.HBM)
    smem = pl.BlockSpec(memory_space=pltpu.SMEM)
    rows = Q * HL
    v = pltpu.VMEM
    dma = pltpu.SemaphoreType.DMA
    scratch = [
        v((rows, queries.shape[2]), BF16),
        v((queries.shape[2], KEYS), BF16),
        v((Q * JL, DI), BF16),
        v((KEYS, DI), BF16),
        v((JL, Q), F32),
        v((QB * HL, KEYS), F32),
        v((QB * HL, KEYS), F32),
        v((QB * HL, 128), F32),
        v((rows, KEYS), F32),
        v((Q * JL, DI), F32),
        v((Q * JL, DI), BF16),
        v((DI, Q * JL), BF16),
        v((DI, KEYS), BF16),
        v((Q * JL, KEYS), F32),
        v((128, 128), F32),
        v((128, 128), F32),
        v((Q * JL, KEYS), BF16),
        v((Q, KEYS), F32), v((32, KEYS), F32), v((32, KEYS), F32), v((Q, KEYS), F32),
        v((2, CH, KEYS), F32), v((2, 16, KEYS), F32), v((2, 16, KEYS), F32), v((2, CH, KEYS), F32),
        v((2, 16, 128), F32), v((2, 7, 16, 128), F32),
        v((2, 16, 128), F32), v((2, 7, 16, 128), F32),
        v((8, 128), F32), v((7, 8, 128), F32), v((8, 128), F32), v((7, 8, 128), F32),
        v((3, 8, 128), F32),
        v((512, DI), F32), v((2, 512, DI), F32), v((2, 7, 64, DI), F32),
        v((2, 64, DI), F32), v((2, NZ, 64, DI), F32),
        v((2, 2, DI, 256), F32), v((2, DI, 256), F32), v((2, DI, 256), F32), v((DI, 256), F32),
        v((2, 64, DI), F32), v((KEYS // 4, DI), F32),
        dma((6,)), dma((11,)), dma((11,)), dma((5, 7)), dma((5, 7)), dma((7, 7)), dma((7, 7)),
    ]
    grad_queries, grad_keys = pl.pallas_call(
        kernel,
        out_shape=(
            jax.ShapeDtypeStruct((Q * JL, DI), F32),
            jax.ShapeDtypeStruct((KEYS // 4, DI), F32),
        ),
        in_specs=[smem] + [hbm] * 5,
        out_specs=(hbm, hbm),
        scratch_shapes=scratch,
        compiler_params=pltpu.CompilerParams(
            collective_id=0, has_side_effects=True, vmem_limit_bytes=63 * 1024 * 1024
        ),
    )(
        positions,
        queries.reshape(rows, queries.shape[2]),
        latents.T,
        index_queries.reshape(Q * JL, DI),
        index_keys,
        index_weights.T,
    )
    return grad_queries.reshape(Q, JL, DI), grad_keys


def solution(mesh):
    placed = (
        P(None, "heads", None),
        P("ctx", None),
        P(None, "heads", None),
        P("ctx", None),
        P(None, "heads"),
        P(),
    )
    return jax.shard_map(
        body,
        mesh=mesh,
        in_specs=placed,
        out_specs=(P(None, "heads", None), P(("ctx", "heads"), None)),
        check_vma=False,
    )
```

```python
import functools

import jax
import jax.numpy as jnp
from jax import lax
from jax.experimental import pallas as pl
from jax.experimental.pallas import tpu as pltpu
from jax.sharding import PartitionSpec as P

MESH = pl.DeviceIdType.MESH
F32 = jnp.float32
BF16 = jnp.bfloat16

Q, H, HI, DI = 64, 128, 64, 128
NZ = 8
NG = 8
HL = 32
JL = 16
KEYS = 1024
QB = 8
NB = Q // QB
CH = 32
LOG2E = 1.4426950408889634
SCORE_SCALE = (192 ** (-0.5)) * LOG2E
INDEX_SCALE = (HI * DI) ** (-0.5)
FILL = -1e30
LOSS_SCALE = 1024.0


def kernel(
    pos_ref, q_hbm, lat_hbm, iq_hbm, ik_hbm, wt_hbm,
    gq_ref, gk_ref,
    q_ref, lat_ref, iq_ref, ik_ref, wt_ref,
    prod_a, prod_b, mb, ex, iqf, iqp, iqt, ikt, dots, wpad, w_ref, coef,
    lg, lg_rc, lg_ry, lg_fin,
    tg, tg_rc, tg_ry, tg_fin,
    st, st_rz, st2, st_rx, ix, ix_rz, ix2, ix_rx, fac,
    gq_tmp, gq, gq_rx, gz, gz_rx,
    gk_p, gk_rc, gk_s, gk_ry, gsum, gk_out,
    load_sem, pair_send, pair_recv, send_z, recv_z, send_x, recv_x,
):
    c = lax.axis_index("ctx")
    h = lax.axis_index("heads")
    z, g = c % NZ, c // NZ
    core, ylo = h % 2, h // 2
    core_peer = (c, ylo * 2 + (1 - core))
    ylo_peer = (c, (1 - ylo) * 2 + core)
    far = (4, 3, 5, 2, 6, 1, 7)
    z_ids = [(z + k) % NZ for k in far]
    g_ids = [(g + k) % NG for k in far]
    z_peers = [(g * NZ + i, h) for i in z_ids]
    g_peers = [(i * NZ + z, h) for i in g_ids]
    peers = z_peers + g_peers + [core_peer, ylo_peer]

    barrier = pltpu.get_barrier_semaphore()
    for p in peers:
        pl.semaphore_signal(barrier, inc=1, device_id=p, device_id_type=MESH)

    def load(k, src, dst):
        copy = pltpu.make_async_copy(src, dst, load_sem.at[k])
        copy.start()
        return copy

    first_rows, last_rows = pl.ds(0, CH * HL), pl.ds(CH * HL, CH * HL)
    l_iq = load(0, iq_hbm, iq_ref)
    l_ik = load(1, ik_hbm, ik_ref)
    l_wt = load(2, wt_hbm, wt_ref)
    l_lat = load(3, lat_hbm, lat_ref)
    l_q0 = load(4, q_hbm.at[first_rows], q_ref.at[first_rows])
    l_q1 = load(5, q_hbm.at[last_rows], q_ref.at[last_rows])

    def remote(src, dst, send, recv, peer):
        return pltpu.make_async_remote_copy(
            src_ref=src, dst_ref=dst, send_sem=send, recv_sem=recv,
            device_id=peer, device_id_type=MESH,
        )

    def pair(slot, src, dst, peer):
        copy = remote(src, dst, pair_send.at[slot], pair_recv.at[slot], peer)
        copy.start()
        return copy

    def spread(slot, sends, recvs, targets, src, dst):
        copies = [
            remote(src(k), dst(k), sends.at[slot, k], recvs.at[slot, k], p)
            for k, p in enumerate(targets)
        ]
        for copy in copies:
            copy.start()
        return copies

    def wait(copies):
        for copy in copies:
            copy.wait()

    lane = lax.broadcasted_iota(jnp.int32, (QB, 128), 1)
    sub = lax.broadcasted_iota(jnp.int32, (QB, 128), 0)
    key_pos = c * KEYS + lane
    row_iota = lax.broadcasted_iota(jnp.int32, (QB, 1), 0)
    GROUPS = KEYS // 128

    def lanes(n):
        return slice(n * 128, (n + 1) * 128)

    def aligned(start, size, by=None):
        return pl.ds(pl.multiple_of(start, by or size), size)

    def tree(op, parts):
        parts = list(parts)
        while len(parts) > 1:
            parts = [op(*parts[i : i + 2]) if i + 1 < len(parts) else parts[i] for i in range(0, len(parts), 2)]
        return parts[0]

    l_iq.wait()
    iqf[...] = iq_ref[...].astype(F32)

    def permute(b, _):
        for j in range(0, JL, 2):
            two = [iqf[pl.ds(b * 128 + j + i, QB, stride=JL), :] for i in range(2)]
            iqp[aligned(b * 128 + j * QB, 2 * QB), :] = jnp.concatenate(two, axis=0).astype(BF16)
        return 0

    lax.fori_loop(0, NB, permute, 0)
    iqt[...] = iqp[...].T
    l_ik.wait()
    ikt[...] = ik_ref[...].T
    l_wt.wait()
    wpad[...] = jnp.zeros_like(wpad)
    wpad[0:JL, 0:Q] = wt_ref[...] * INDEX_SCALE
    w_ref[...] = wpad[...].T

    for n in range(KEYS // 256):
        at = slice(n * 256, (n + 1) * 256)
        dots[:, at] = jnp.dot(iqp[...], ikt[:, at], preferred_element_type=F32)

    def index_block(b, _):
        wb = w_ref[aligned(b * QB, QB), :]
        ws = [jnp.broadcast_to(wb[:, j : j + 1], (QB, 128)) for j in range(JL)]
        col = jnp.zeros((QB, 1), jnp.int32)
        for i in range(QB):
            col = jnp.where(row_iota == i, pos_ref[b * QB + i], col)
        col = jnp.broadcast_to(col, (QB, 128))
        for n in range(GROUPS):
            total = tree(jnp.add, [
                ws[j] * jnp.maximum(dots[aligned(b * 128 + j * QB, QB), lanes(n)], 0.0)
                for j in range(JL)
            ])
            lg[aligned(b * QB, QB), lanes(n)] = jnp.where(key_pos + n * 128 <= col, total, FILL)
        return 0

    lax.fori_loop(0, NB, index_block, 0, unroll=True)

    def multiply(b, prod):
        rows = aligned(b * (QB * HL), QB * HL)
        for n in range(KEYS // 256):
            at = slice(n * 256, (n + 1) * 256)
            prod[:, at] = jnp.dot(q_ref[rows, :], lat_ref[:, at], preferred_element_type=F32)

    def softmax(b, prod, carry):
        local = b % (CH // QB) * QB

        def peaks(k, ms):
            pos = pos_ref[b * QB + k]
            vis = [key_pos + n * 128 <= pos for n in range(GROUPS)]
            for i in range(HL // QB):
                rows = aligned(k * HL + i * QB, QB)
                m = tree(jnp.maximum, [
                    jnp.where(vis[n], prod[rows, lanes(n)], FILL) for n in range(GROUPS)
                ])
                m = jnp.broadcast_to(jnp.max(m, axis=1, keepdims=True) * SCORE_SCALE, (QB, 128))
                mb[rows, :] = m
                ms = jnp.where(lane == i * 32 + local + k, m, ms)
            return ms

        def masses(k, ls):
            pos = pos_ref[b * QB + k]
            vis = [key_pos + n * 128 <= pos for n in range(GROUPS)]
            for i in range(HL // QB):
                rows = aligned(k * HL + i * QB, QB)
                m = mb[rows, :]
                to = aligned(b * (QB * HL) + k * HL + i * QB, QB)
                es = []
                for n in range(GROUPS):
                    e = jnp.exp2(prod[rows, lanes(n)] * SCORE_SCALE - m)
                    e = jnp.where(vis[n], e, 0.0)
                    ex[to, lanes(n)] = e
                    es.append(e)
                l = jnp.sum(tree(jnp.add, es), axis=1, keepdims=True)
                ls = jnp.where(lane == i * 32 + local + k, l, ls)
            return ls

        ms = lax.fori_loop(0, QB, peaks, carry[0], unroll=True)
        ls = lax.fori_loop(0, QB, masses, carry[1], unroll=True)
        return ms, ls

    def two_blocks(i, carry):
        multiply(2 * i + 1, prod_b)
        carry = softmax(2 * i, prod_a, carry)
        multiply(jnp.minimum(2 * i + 2, NB - 1), prod_a)
        return softmax(2 * i + 1, prod_b, carry)

    def attention(first, last, carry):
        return lax.fori_loop(first, last, two_blocks, carry)

    zero = jnp.zeros((QB, 128), F32)
    half = aligned(core * 32, 32)
    other = aligned((1 - core) * 32, 32)

    l_lat.wait()
    l_q0.wait()
    multiply(0, prod_a)
    l_q1.wait()
    ms, ls = attention(0, 2, (zero, zero))
    st[0, 0:8, :] = ms
    st[0, 8:16, :] = ls
    pl.semaphore_wait(barrier, len(peers))
    s_z0 = spread(0, send_z, recv_z, z_peers, lambda k: st.at[0], lambda k: st_rz.at[0, k])
    lg1 = pair(0, lg.at[other], lg_rc, core_peer)
    carry = attention(2, 3, (zero, zero))
    lg1.wait()
    lg[half, :] = lg[half, :] + lg_rc[...]
    lg2 = pair(1, lg.at[half], lg_ry, ylo_peer)
    ms, ls = attention(3, 4, carry)
    st[1, 0:8, :] = ms
    st[1, 8:16, :] = ls
    s_z1 = spread(1, send_z, recv_z, z_peers, lambda k: st.at[1], lambda k: st_rz.at[1, k])

    def index_stats(b, so_far):
        rows = aligned(b * QB, QB)
        xs = [lg_fin[rows, lanes(n)] * LOG2E for n in range(GROUPS)]
        m = jnp.max(tree(jnp.maximum, xs), axis=1, keepdims=True)
        mm = jnp.broadcast_to(m, (QB, 128))
        l = jnp.sum(tree(jnp.add, [jnp.exp2(x - mm) for x in xs]), axis=1, keepdims=True)
        return jnp.where(lane == b, m, jnp.where(lane == b + 64, l, so_far))

    def combine(own, received):
        parts = [own[...]] + [received[k] for k in range(7)]
        top = tree(jnp.maximum, [p[0:8] for p in parts])
        mass = tree(jnp.add, [p[8:16] * jnp.exp2(p[0:8] - top) for p in parts])
        return top, mass

    def combine_index(own, received):
        parts = [own[...]] + [received[k] for k in range(7)]
        peak = tree(jnp.maximum, parts)
        low = lane < 64
        mass = tree(jnp.add, [
            p * pltpu.roll(jnp.exp2(jnp.where(low, p - peak, 0.0)), 64, 1) for p in parts
        ])
        return jnp.where(low, peak, mass)

    def combined_z(t):
        top, mass = combine(st.at[t], st_rz.at[t])
        st2[t, 0:8, :] = top
        st2[t, 8:16, :] = mass
        return spread(t, send_x, recv_x, g_peers, lambda k: st2.at[t], lambda k: st_rx.at[t, k])

    def factors(t):
        top, mass = combine(st2.at[t], st_rx.at[t])
        fac[t] = jnp.exp2(st[t, 0:8, :] - top) / mass

    def turn(x, shift):
        return pltpu.roll(x, shift % QB, 0)

    def gathered(r):
        r = [r[i] for i in (3, 2, 1, 0, 7, 6, 5, 4)]
        low = sub < 4
        a = [
            jnp.where(low, r[i], r[i + 4]) + turn(jnp.where(low, r[i + 4], r[i]), 4)
            for i in range(4)
        ]
        low = sub % 4 < 2
        b = [jnp.where(low, a[i + 2] + turn(a[i + 2], -2), a[i] + turn(a[i], 2)) for i in range(2)]
        return jnp.where(sub % 2 < 1, b[1] + turn(b[1], -1), b[0] + turn(b[0], 1))

    def target(t):
        f = fac[t]
        for b in range(CH // QB):
            fs = [
                [
                    jnp.broadcast_to(f[:, i * 32 + b * QB + k : i * 32 + b * QB + k + 1], (QB, 128))
                    for i in range(4)
                ]
                for k in range(QB)
            ]
            for n in range(GROUPS):
                r = []
                for k in range(QB):
                    at = (t * (CH // QB) + b) * (QB * HL) + k * HL
                    r.append(tree(jnp.add, [
                        ex[at + i * QB : at + (i + 1) * QB, lanes(n)] * fs[k][i] for i in range(4)
                    ]))
                tg[t, b * QB : (b + 1) * QB, lanes(n)] = gathered(r)

    part = aligned(core * 16, 16)
    other_part = aligned((1 - core) * 16, 16)

    def core_one(t):
        return pair(3 + t, tg.at[t, other_part], tg_rc.at[t], core_peer)

    def across(t):
        tg[t, part, :] = tg[t, part, :] + tg_rc[t]
        return pair(5 + t, tg.at[t, part], tg_ry.at[t], ylo_peer)

    def core_two(t):
        tg_fin[t, part, :] = tg[t, part, :] + tg_ry[t]
        return pair(7 + t, tg_fin.at[t, part], tg_fin.at[t, part], core_peer)

    def grads(t):
        totals = fac[2]
        for i in range(CH // QB):
            b = t * (CH // QB) + i
            rows = slice(b * QB, (b + 1) * QB)
            peak = jnp.broadcast_to(totals[:, b : b + 1], (QB, 128))
            share = jnp.broadcast_to(LOSS_SCALE / totals[:, b + 64 : b + 65], (QB, 128))
            wb = w_ref[rows, :]
            ws = [jnp.broadcast_to(wb[:, j : j + 1], (QB, 128)) for j in range(JL)]
            for n in range(GROUPS):
                probs = jnp.exp2(lg_fin[rows, lanes(n)] * LOG2E - peak) * share
                grad = probs - tg_fin[t, i * QB : (i + 1) * QB, lanes(n)] * (LOSS_SCALE / H)
                for j in range(0, JL, 2):
                    two = []
                    for jj in (j, j + 1):
                        d = dots[b * 128 + jj * QB : b * 128 + (jj + 1) * QB, lanes(n)]
                        two.append(jnp.where(d > 0.0, grad * ws[jj], 0.0))
                    at = slice(b * 128 + j * QB, b * 128 + (j + 2) * QB)
                    coef[at, lanes(n)] = jnp.concatenate(two, axis=0).astype(BF16)
        gq_tmp[...] = jnp.dot(
            coef[t * 512 : (t + 1) * 512, :], ik_ref[...], preferred_element_type=F32
        )
        for i in range(CH // QB):
            for k in range(QB):
                gq[t, i * 128 + k * JL : i * 128 + (k + 1) * JL, :] = gq_tmp[
                    pl.ds(i * 128 + k, JL, stride=QB), :
                ]
        return spread(
            2 + t, send_x, recv_x, g_peers,
            lambda k: gq.at[t, aligned(g_ids[k] * 64, 64)], lambda k: gq_rx.at[t, k],
        )

    def sum_x(t):
        mine = gq[t, aligned(g * 64, 64), :]
        gz[t] = tree(jnp.add, [mine] + [gq_rx[t, k] for k in range(7)])
        gz_rx[t, z] = gz[t]
        return spread(
            2 + t, send_z, recv_z, z_peers, lambda k: gz.at[t], lambda k: gz_rx.at[t, z]
        )

    def sum_z(t):
        mine = aligned(t * 512 + g * 64, 64)
        gsum[t] = tree(jnp.add, [gz_rx[t, k] for k in range(NZ)])
        copies = spread(
            4 + t, send_x, recv_x, g_peers, lambda k: gsum.at[t], lambda k: gq_ref.at[mine]
        )
        return copies + [load(t, gsum.at[t], gq_ref.at[mine])]

    wait(s_z0)
    s_x0 = combined_z(0)
    lg2.wait()
    lg_fin[half, :] = lg[half, :] + lg_ry[...]
    lg3 = pair(2, lg_fin.at[half], lg_fin.at[half], core_peer)
    lg3.wait()
    ix[...] = lax.fori_loop(0, NB, index_stats, zero, unroll=True)
    i_z = spread(4, send_z, recv_z, z_peers, lambda k: ix, lambda k: ix_rz.at[k])
    wait(s_z1)
    s_x1 = combined_z(1)
    wait(s_x0)
    factors(0)
    target(0)
    one0 = core_one(0)
    wait(i_z)
    ix2[...] = combine_index(ix, ix_rz)
    i_x = spread(6, send_x, recv_x, g_peers, lambda k: ix2, lambda k: ix_rx.at[k])
    one0.wait()
    across0 = across(0)
    wait(s_x1)
    factors(1)
    target(1)
    one1 = core_one(1)
    across0.wait()
    two0 = core_two(0)
    one1.wait()
    across1 = across(1)
    wait(i_x)
    fac[2] = combine_index(ix2, ix_rx)
    two0.wait()
    rs0 = grads(0)
    across1.wait()
    two1 = core_two(1)
    two1.wait()
    rs1 = grads(1)

    for piece in range(4):
        gk_p[piece % 2, piece // 2] = jnp.dot(
            iqt[...], coef[:, piece * 256 : (piece + 1) * 256], preferred_element_type=F32
        )
    gk1 = pair(9, gk_p.at[1 - core], gk_rc, core_peer)
    wait(rs0)
    sz0 = sum_x(0)
    gk1.wait()
    gk_s[...] = gk_p[core] + gk_rc[...]
    gk2 = pair(10, gk_s.at[1 - ylo], gk_ry, ylo_peer)
    wait(rs1)
    sz1 = sum_x(1)
    gk2.wait()
    gk_out[...] = (gk_s[ylo] + gk_ry[...]).T
    gk_store = load(2, gk_out, gk_ref)
    wait(sz0)
    ag0 = sum_z(0)
    wait(sz1)
    ag1 = sum_z(1)
    wait(ag0)
    wait(ag1)
    gk_store.wait()


def deliver(gq_in, gk_in, gq_out, gk_out, gq_buf, gk_buf, arrive, leave):
    part = Q * JL // 4

    def piece(k):
        return pl.ds(k * part, part)

    first = [pltpu.make_async_copy(gk_in, gk_buf, arrive.at[4])]
    last = [pltpu.make_async_copy(gk_buf, gk_out, leave.at[4])]
    for k in range(4):
        first.append(pltpu.make_async_copy(gq_in.at[piece(k)], gq_buf.at[piece(k)], arrive.at[k]))
        last.append(pltpu.make_async_copy(gq_buf.at[piece(k)], gq_out.at[piece(k)], leave.at[k]))
    for copy in first:
        copy.start()
    for one, two in zip(first, last):
        one.wait()
        two.start()
    for copy in last:
        copy.wait()


def body(queries, latents, index_queries, index_keys, index_weights, positions):
    hbm = pl.BlockSpec(memory_space=pltpu.HBM)
    smem = pl.BlockSpec(memory_space=pltpu.SMEM)
    rows = Q * HL
    v = pltpu.VMEM
    dma = pltpu.SemaphoreType.DMA
    scratch = [
        v((rows, queries.shape[2]), BF16),
        v((queries.shape[2], KEYS), BF16),
        v((Q * JL, DI), BF16),
        v((KEYS, DI), BF16),
        v((JL, Q), F32),
        v((QB * HL, KEYS), F32),
        v((QB * HL, KEYS), F32),
        v((QB * HL, 128), F32),
        v((rows, KEYS), F32),
        v((Q * JL, DI), F32),
        v((Q * JL, DI), BF16),
        v((DI, Q * JL), BF16),
        v((DI, KEYS), BF16),
        v((Q * JL, KEYS), F32),
        v((128, 128), F32),
        v((128, 128), F32),
        v((Q * JL, KEYS), BF16),
        v((Q, KEYS), F32), v((32, KEYS), F32), v((32, KEYS), F32), v((Q, KEYS), F32),
        v((2, CH, KEYS), F32), v((2, 16, KEYS), F32), v((2, 16, KEYS), F32), v((2, CH, KEYS), F32),
        v((2, 16, 128), F32), v((2, 7, 16, 128), F32),
        v((2, 16, 128), F32), v((2, 7, 16, 128), F32),
        v((8, 128), F32), v((7, 8, 128), F32), v((8, 128), F32), v((7, 8, 128), F32),
        v((3, 8, 128), F32),
        v((512, DI), F32), v((2, 512, DI), F32), v((2, 7, 64, DI), F32),
        v((2, 64, DI), F32), v((2, NZ, 64, DI), F32),
        v((2, 2, DI, 256), F32), v((2, DI, 256), F32), v((2, DI, 256), F32), v((DI, 256), F32),
        v((2, 64, DI), F32), v((KEYS // 4, DI), F32),
        dma((6,)), dma((11,)), dma((11,)), dma((5, 7)), dma((5, 7)), dma((7, 7)), dma((7, 7)),
    ]
    grad_queries, grad_keys = pl.pallas_call(
        kernel,
        out_shape=(
            jax.ShapeDtypeStruct((Q * JL, DI), F32),
            jax.ShapeDtypeStruct((KEYS // 4, DI), F32),
        ),
        in_specs=[smem] + [hbm] * 5,
        out_specs=(hbm, hbm),
        scratch_shapes=scratch,
        compiler_params=pltpu.CompilerParams(
            collective_id=0, has_side_effects=True, vmem_limit_bytes=63 * 1024 * 1024
        ),
    )(
        positions,
        queries.reshape(rows, queries.shape[2]),
        latents.T,
        index_queries.reshape(Q * JL, DI),
        index_keys,
        index_weights.T,
    )
    grad_queries, grad_keys = pl.pallas_call(
        deliver,
        out_shape=(
            jax.ShapeDtypeStruct((Q * JL, DI), F32),
            jax.ShapeDtypeStruct((KEYS // 4, DI), F32),
        ),
        in_specs=[hbm, hbm],
        out_specs=(hbm, hbm),
        scratch_shapes=[v((Q * JL, DI), F32), v((KEYS // 4, DI), F32), dma((5,)), dma((5,))],
        compiler_params=pltpu.CompilerParams(vmem_limit_bytes=63 * 1024 * 1024),
    )(grad_queries, grad_keys)
    return grad_queries.reshape(Q, JL, DI), grad_keys


def solution(mesh):
    placed = (
        P(None, "heads", None),
        P("ctx", None),
        P(None, "heads", None),
        P("ctx", None),
        P(None, "heads"),
        P(),
    )
    return jax.shard_map(
        body,
        mesh=mesh,
        in_specs=placed,
        out_specs=(P(None, "heads", None), P(("ctx", "heads"), None)),
        check_vma=False,
    )
```

```python
import functools

import jax
import jax.numpy as jnp
from jax import lax
from jax.experimental import pallas as pl
from jax.experimental.pallas import tpu as pltpu
from jax.sharding import PartitionSpec as P

MESH = pl.DeviceIdType.MESH
F32 = jnp.float32
BF16 = jnp.bfloat16

Q, H, HI, DI = 64, 128, 64, 128
NZ = 8
NG = 8
HL = 32
JL = 16
KEYS = 1024
QB = 8
NB = Q // QB
CH = 32
LOG2E = 1.4426950408889634
SCORE_SCALE = (192 ** (-0.5)) * LOG2E
INDEX_SCALE = (HI * DI) ** (-0.5)
FILL = -1e30
LOSS_SCALE = 1024.0


def kernel(
    pos_ref, q_hbm, lat_hbm, iq_hbm, ik_hbm, wt_hbm,
    gq_ref, gk_ref,
    q_ref, lat_ref, iq_ref, ik_ref, wt_ref,
    prod_a, prod_b, mb, ex, iqf, iqp, iqt, ikt, dots, wpad, w_ref, coef,
    lg, lg_rc, lg_ry, lg_fin,
    tg, tg_rc, tg_ry, tg_fin,
    st, st_rz, st2, st_rx, ix, ix_rz, ix2, ix_rx, fac,
    gq_tmp, gq, gq_rx, gz, gz_rx,
    gk_p, gk_rc, gk_s, gk_ry, gsum, gk_out,
    load_sem, pair_send, pair_recv, send_z, recv_z, send_x, recv_x,
):
    c = lax.axis_index("ctx")
    h = lax.axis_index("heads")
    z, g = c % NZ, c // NZ
    core, ylo = h % 2, h // 2
    core_peer = (c, ylo * 2 + (1 - core))
    ylo_peer = (c, (1 - ylo) * 2 + core)
    far = (4, 3, 5, 2, 6, 1, 7)
    z_ids = [(z + k) % NZ for k in far]
    g_ids = [(g + k) % NG for k in far]
    z_peers = [(g * NZ + i, h) for i in z_ids]
    g_peers = [(i * NZ + z, h) for i in g_ids]
    peers = z_peers + g_peers + [core_peer, ylo_peer]

    barrier = pltpu.get_barrier_semaphore()
    for p in peers:
        pl.semaphore_signal(barrier, inc=1, device_id=p, device_id_type=MESH)

    def load(k, src, dst):
        copy = pltpu.make_async_copy(src, dst, load_sem.at[k])
        copy.start()
        return copy

    first_rows, last_rows = pl.ds(0, CH * HL), pl.ds(CH * HL, CH * HL)
    l_iq = load(0, iq_hbm, iq_ref)
    l_ik = load(1, ik_hbm, ik_ref)
    l_wt = load(2, wt_hbm, wt_ref)
    l_lat = load(3, lat_hbm, lat_ref)
    l_q0 = load(4, q_hbm.at[first_rows], q_ref.at[first_rows])
    l_q1 = load(5, q_hbm.at[last_rows], q_ref.at[last_rows])

    def remote(src, dst, send, recv, peer):
        return pltpu.make_async_remote_copy(
            src_ref=src, dst_ref=dst, send_sem=send, recv_sem=recv,
            device_id=peer, device_id_type=MESH,
        )

    def pair(slot, src, dst, peer):
        copy = remote(src, dst, pair_send.at[slot], pair_recv.at[slot], peer)
        copy.start()
        return copy

    def spread(slot, sends, recvs, targets, src, dst):
        copies = [
            remote(src(k), dst(k), sends.at[slot, k], recvs.at[slot, k], p)
            for k, p in enumerate(targets)
        ]
        for copy in copies:
            copy.start()
        return copies

    def wait(copies):
        for copy in copies:
            copy.wait()

    lane = lax.broadcasted_iota(jnp.int32, (QB, 128), 1)
    sub = lax.broadcasted_iota(jnp.int32, (QB, 128), 0)
    key_pos = c * KEYS + lane
    row_iota = lax.broadcasted_iota(jnp.int32, (QB, 1), 0)
    GROUPS = KEYS // 128

    def lanes(n):
        return slice(n * 128, (n + 1) * 128)

    def aligned(start, size, by=None):
        return pl.ds(pl.multiple_of(start, by or size), size)

    def tree(op, parts):
        parts = list(parts)
        while len(parts) > 1:
            parts = [op(*parts[i : i + 2]) if i + 1 < len(parts) else parts[i] for i in range(0, len(parts), 2)]
        return parts[0]

    l_iq.wait()
    iqf[...] = iq_ref[...].astype(F32)

    def permute(b, _):
        for j in range(0, JL, 2):
            two = [iqf[pl.ds(b * 128 + j + i, QB, stride=JL), :] for i in range(2)]
            iqp[aligned(b * 128 + j * QB, 2 * QB), :] = jnp.concatenate(two, axis=0).astype(BF16)
        return 0

    lax.fori_loop(0, NB, permute, 0)
    iqt[...] = iqp[...].T
    l_ik.wait()
    ikt[...] = ik_ref[...].T
    l_wt.wait()
    wpad[...] = jnp.zeros_like(wpad)
    wpad[0:JL, 0:Q] = wt_ref[...] * INDEX_SCALE
    w_ref[...] = wpad[...].T

    for n in range(KEYS // 256):
        at = slice(n * 256, (n + 1) * 256)
        dots[:, at] = jnp.dot(iqp[...], ikt[:, at], preferred_element_type=F32)

    def index_block(b, _):
        wb = w_ref[aligned(b * QB, QB), :]
        ws = [jnp.broadcast_to(wb[:, j : j + 1], (QB, 128)) for j in range(JL)]
        col = jnp.zeros((QB, 1), jnp.int32)
        for i in range(QB):
            col = jnp.where(row_iota == i, pos_ref[b * QB + i], col)
        col = jnp.broadcast_to(col, (QB, 128))
        for n in range(GROUPS):
            total = tree(jnp.add, [
                ws[j] * jnp.maximum(dots[aligned(b * 128 + j * QB, QB), lanes(n)], 0.0)
                for j in range(JL)
            ])
            lg[aligned(b * QB, QB), lanes(n)] = jnp.where(key_pos + n * 128 <= col, total, FILL)
        return 0

    lax.fori_loop(0, NB, index_block, 0, unroll=True)

    def multiply(b, prod):
        rows = aligned(b * (QB * HL), QB * HL)
        for n in range(KEYS // 256):
            at = slice(n * 256, (n + 1) * 256)
            prod[:, at] = jnp.dot(q_ref[rows, :], lat_ref[:, at], preferred_element_type=F32)

    def softmax(b, prod, carry):
        local = b % (CH // QB) * QB

        def peaks(k, ms):
            pos = pos_ref[b * QB + k]
            vis = [key_pos + n * 128 <= pos for n in range(GROUPS)]
            for i in range(HL // QB):
                rows = aligned(k * HL + i * QB, QB)
                m = tree(jnp.maximum, [
                    jnp.where(vis[n], prod[rows, lanes(n)], FILL) for n in range(GROUPS)
                ])
                m = jnp.broadcast_to(jnp.max(m, axis=1, keepdims=True) * SCORE_SCALE, (QB, 128))
                mb[rows, :] = m
                ms = jnp.where(lane == i * 32 + local + k, m, ms)
            return ms

        def masses(k, ls):
            pos = pos_ref[b * QB + k]
            vis = [key_pos + n * 128 <= pos for n in range(GROUPS)]
            for i in range(HL // QB):
                rows = aligned(k * HL + i * QB, QB)
                m = mb[rows, :]
                to = aligned(b * (QB * HL) + k * HL + i * QB, QB)
                es = []
                for n in range(GROUPS):
                    e = jnp.exp2(prod[rows, lanes(n)] * SCORE_SCALE - m)
                    e = jnp.where(vis[n], e, 0.0)
                    ex[to, lanes(n)] = e
                    es.append(e)
                l = jnp.sum(tree(jnp.add, es), axis=1, keepdims=True)
                ls = jnp.where(lane == i * 32 + local + k, l, ls)
            return ls

        ms = lax.fori_loop(0, QB, peaks, carry[0], unroll=True)
        ls = lax.fori_loop(0, QB, masses, carry[1], unroll=True)
        return ms, ls

    def two_blocks(i, carry):
        multiply(2 * i + 1, prod_b)
        carry = softmax(2 * i, prod_a, carry)
        multiply(jnp.minimum(2 * i + 2, NB - 1), prod_a)
        return softmax(2 * i + 1, prod_b, carry)

    def attention(first, last, carry):
        return lax.fori_loop(first, last, two_blocks, carry)

    zero = jnp.zeros((QB, 128), F32)
    half = aligned(core * 32, 32)
    other = aligned((1 - core) * 32, 32)

    l_lat.wait()
    l_q0.wait()
    multiply(0, prod_a)
    l_q1.wait()
    for t in range(2):
        ms, ls = attention(2 * t, 2 * t + 2, (zero, zero))
        st[t, 0:8, :] = ms
        st[t, 8:16, :] = ls
    pl.semaphore_wait(barrier, len(peers))
    s_z0 = spread(0, send_z, recv_z, z_peers, lambda k: st.at[0], lambda k: st_rz.at[0, k])
    lg1 = pair(0, lg.at[other], lg_rc, core_peer)
    s_z1 = spread(1, send_z, recv_z, z_peers, lambda k: st.at[1], lambda k: st_rz.at[1, k])
    lg1.wait()
    lg[half, :] = lg[half, :] + lg_rc[...]
    lg2 = pair(1, lg.at[half], lg_ry, ylo_peer)

    def index_stats(b, so_far):
        rows = aligned(b * QB, QB)
        xs = [lg_fin[rows, lanes(n)] * LOG2E for n in range(GROUPS)]
        m = jnp.max(tree(jnp.maximum, xs), axis=1, keepdims=True)
        mm = jnp.broadcast_to(m, (QB, 128))
        l = jnp.sum(tree(jnp.add, [jnp.exp2(x - mm) for x in xs]), axis=1, keepdims=True)
        return jnp.where(lane == b, m, jnp.where(lane == b + 64, l, so_far))

    def combine(own, received):
        parts = [own[...]] + [received[k] for k in range(7)]
        top = tree(jnp.maximum, [p[0:8] for p in parts])
        mass = tree(jnp.add, [p[8:16] * jnp.exp2(p[0:8] - top) for p in parts])
        return top, mass

    def combine_index(own, received):
        parts = [own[...]] + [received[k] for k in range(7)]
        peak = tree(jnp.maximum, parts)
        low = lane < 64
        mass = tree(jnp.add, [
            p * pltpu.roll(jnp.exp2(jnp.where(low, p - peak, 0.0)), 64, 1) for p in parts
        ])
        return jnp.where(low, peak, mass)

    def combined_z(t):
        top, mass = combine(st.at[t], st_rz.at[t])
        st2[t, 0:8, :] = top
        st2[t, 8:16, :] = mass
        return spread(t, send_x, recv_x, g_peers, lambda k: st2.at[t], lambda k: st_rx.at[t, k])

    def factors(t):
        top, mass = combine(st2.at[t], st_rx.at[t])
        fac[t] = jnp.exp2(st[t, 0:8, :] - top) / mass

    def turn(x, shift):
        return pltpu.roll(x, shift % QB, 0)

    def gathered(r):
        r = [r[i] for i in (3, 2, 1, 0, 7, 6, 5, 4)]
        low = sub < 4
        a = [
            jnp.where(low, r[i], r[i + 4]) + turn(jnp.where(low, r[i + 4], r[i]), 4)
            for i in range(4)
        ]
        low = sub % 4 < 2
        b = [jnp.where(low, a[i + 2] + turn(a[i + 2], -2), a[i] + turn(a[i], 2)) for i in range(2)]
        return jnp.where(sub % 2 < 1, b[1] + turn(b[1], -1), b[0] + turn(b[0], 1))

    def target(t):
        f = fac[t]
        for b in range(CH // QB):
            fs = [
                [
                    jnp.broadcast_to(f[:, i * 32 + b * QB + k : i * 32 + b * QB + k + 1], (QB, 128))
                    for i in range(4)
                ]
                for k in range(QB)
            ]
            for n in range(GROUPS):
                r = []
                for k in range(QB):
                    at = (t * (CH // QB) + b) * (QB * HL) + k * HL
                    r.append(tree(jnp.add, [
                        ex[at + i * QB : at + (i + 1) * QB, lanes(n)] * fs[k][i] for i in range(4)
                    ]))
                tg[t, b * QB : (b + 1) * QB, lanes(n)] = gathered(r)

    part = aligned(core * 16, 16)
    other_part = aligned((1 - core) * 16, 16)

    def core_one(t):
        return pair(3 + t, tg.at[t, other_part], tg_rc.at[t], core_peer)

    def across(t):
        tg[t, part, :] = tg[t, part, :] + tg_rc[t]
        return pair(5 + t, tg.at[t, part], tg_ry.at[t], ylo_peer)

    def core_two(t):
        tg_fin[t, part, :] = tg[t, part, :] + tg_ry[t]
        return pair(7 + t, tg_fin.at[t, part], tg_fin.at[t, part], core_peer)

    def grads(t):
        totals = fac[2]
        for i in range(CH // QB):
            b = t * (CH // QB) + i
            rows = slice(b * QB, (b + 1) * QB)
            peak = jnp.broadcast_to(totals[:, b : b + 1], (QB, 128))
            share = jnp.broadcast_to(LOSS_SCALE / totals[:, b + 64 : b + 65], (QB, 128))
            wb = w_ref[rows, :]
            ws = [jnp.broadcast_to(wb[:, j : j + 1], (QB, 128)) for j in range(JL)]
            for n in range(GROUPS):
                probs = jnp.exp2(lg_fin[rows, lanes(n)] * LOG2E - peak) * share
                grad = probs - tg_fin[t, i * QB : (i + 1) * QB, lanes(n)] * (LOSS_SCALE / H)
                for j in range(0, JL, 2):
                    two = []
                    for jj in (j, j + 1):
                        d = dots[b * 128 + jj * QB : b * 128 + (jj + 1) * QB, lanes(n)]
                        two.append(jnp.where(d > 0.0, grad * ws[jj], 0.0))
                    at = slice(b * 128 + j * QB, b * 128 + (j + 2) * QB)
                    coef[at, lanes(n)] = jnp.concatenate(two, axis=0).astype(BF16)
        gq_tmp[...] = jnp.dot(
            coef[t * 512 : (t + 1) * 512, :], ik_ref[...], preferred_element_type=F32
        )
        for i in range(CH // QB):
            for k in range(QB):
                gq[t, i * 128 + k * JL : i * 128 + (k + 1) * JL, :] = gq_tmp[
                    pl.ds(i * 128 + k, JL, stride=QB), :
                ]
        return spread(
            2 + t, send_x, recv_x, g_peers,
            lambda k: gq.at[t, aligned(g_ids[k] * 64, 64)], lambda k: gq_rx.at[t, k],
        )

    def sum_x(t):
        mine = gq[t, aligned(g * 64, 64), :]
        gz[t] = tree(jnp.add, [mine] + [gq_rx[t, k] for k in range(7)])
        gz_rx[t, z] = gz[t]
        return spread(
            2 + t, send_z, recv_z, z_peers, lambda k: gz.at[t], lambda k: gz_rx.at[t, z]
        )

    def sum_z(t):
        mine = aligned(t * 512 + g * 64, 64)
        gsum[t] = tree(jnp.add, [gz_rx[t, k] for k in range(NZ)])
        copies = spread(
            4 + t, send_x, recv_x, g_peers, lambda k: gsum.at[t], lambda k: gq_ref.at[mine]
        )
        return copies + [load(t, gsum.at[t], gq_ref.at[mine])]

    wait(s_z0)
    s_x0 = combined_z(0)
    lg2.wait()
    lg_fin[half, :] = lg[half, :] + lg_ry[...]
    lg3 = pair(2, lg_fin.at[half], lg_fin.at[half], core_peer)
    lg3.wait()
    ix[...] = lax.fori_loop(0, NB, index_stats, zero, unroll=True)
    i_z = spread(4, send_z, recv_z, z_peers, lambda k: ix, lambda k: ix_rz.at[k])
    wait(s_z1)
    s_x1 = combined_z(1)
    wait(s_x0)
    factors(0)
    target(0)
    one0 = core_one(0)
    wait(i_z)
    ix2[...] = combine_index(ix, ix_rz)
    i_x = spread(6, send_x, recv_x, g_peers, lambda k: ix2, lambda k: ix_rx.at[k])
    one0.wait()
    across0 = across(0)
    wait(s_x1)
    factors(1)
    target(1)
    one1 = core_one(1)
    across0.wait()
    two0 = core_two(0)
    one1.wait()
    across1 = across(1)
    wait(i_x)
    fac[2] = combine_index(ix2, ix_rx)
    two0.wait()
    rs0 = grads(0)
    across1.wait()
    two1 = core_two(1)
    two1.wait()
    rs1 = grads(1)

    for piece in range(4):
        gk_p[piece % 2, piece // 2] = jnp.dot(
            iqt[...], coef[:, piece * 256 : (piece + 1) * 256], preferred_element_type=F32
        )
    gk1 = pair(9, gk_p.at[1 - core], gk_rc, core_peer)
    wait(rs0)
    sz0 = sum_x(0)
    gk1.wait()
    gk_s[...] = gk_p[core] + gk_rc[...]
    gk2 = pair(10, gk_s.at[1 - ylo], gk_ry, ylo_peer)
    wait(rs1)
    sz1 = sum_x(1)
    gk2.wait()
    gk_out[...] = (gk_s[ylo] + gk_ry[...]).T
    gk_store = load(2, gk_out, gk_ref)
    wait(sz0)
    ag0 = sum_z(0)
    wait(sz1)
    ag1 = sum_z(1)
    wait(ag0)
    wait(ag1)
    gk_store.wait()


def deliver(gq_in, gk_in, gq_out, gk_out, gq_buf, gk_buf, arrive, leave):
    part = Q * JL // 4

    def piece(k):
        return pl.ds(k * part, part)

    first = [pltpu.make_async_copy(gk_in, gk_buf, arrive.at[4])]
    last = [pltpu.make_async_copy(gk_buf, gk_out, leave.at[4])]
    for k in range(4):
        first.append(pltpu.make_async_copy(gq_in.at[piece(k)], gq_buf.at[piece(k)], arrive.at[k]))
        last.append(pltpu.make_async_copy(gq_buf.at[piece(k)], gq_out.at[piece(k)], leave.at[k]))
    for copy in first:
        copy.start()
    for one, two in zip(first, last):
        one.wait()
        two.start()
    for copy in last:
        copy.wait()


def body(queries, latents, index_queries, index_keys, index_weights, positions):
    hbm = pl.BlockSpec(memory_space=pltpu.HBM)
    smem = pl.BlockSpec(memory_space=pltpu.SMEM)
    rows = Q * HL
    v = pltpu.VMEM
    dma = pltpu.SemaphoreType.DMA
    scratch = [
        v((rows, queries.shape[2]), BF16),
        v((queries.shape[2], KEYS), BF16),
        v((Q * JL, DI), BF16),
        v((KEYS, DI), BF16),
        v((JL, Q), F32),
        v((QB * HL, KEYS), F32),
        v((QB * HL, KEYS), F32),
        v((QB * HL, 128), F32),
        v((rows, KEYS), F32),
        v((Q * JL, DI), F32),
        v((Q * JL, DI), BF16),
        v((DI, Q * JL), BF16),
        v((DI, KEYS), BF16),
        v((Q * JL, KEYS), F32),
        v((128, 128), F32),
        v((128, 128), F32),
        v((Q * JL, KEYS), BF16),
        v((Q, KEYS), F32), v((32, KEYS), F32), v((32, KEYS), F32), v((Q, KEYS), F32),
        v((2, CH, KEYS), F32), v((2, 16, KEYS), F32), v((2, 16, KEYS), F32), v((2, CH, KEYS), F32),
        v((2, 16, 128), F32), v((2, 7, 16, 128), F32),
        v((2, 16, 128), F32), v((2, 7, 16, 128), F32),
        v((8, 128), F32), v((7, 8, 128), F32), v((8, 128), F32), v((7, 8, 128), F32),
        v((3, 8, 128), F32),
        v((512, DI), F32), v((2, 512, DI), F32), v((2, 7, 64, DI), F32),
        v((2, 64, DI), F32), v((2, NZ, 64, DI), F32),
        v((2, 2, DI, 256), F32), v((2, DI, 256), F32), v((2, DI, 256), F32), v((DI, 256), F32),
        v((2, 64, DI), F32), v((KEYS // 4, DI), F32),
        dma((6,)), dma((11,)), dma((11,)), dma((5, 7)), dma((5, 7)), dma((7, 7)), dma((7, 7)),
    ]
    grad_queries, grad_keys = pl.pallas_call(
        kernel,
        out_shape=(
            jax.ShapeDtypeStruct((Q * JL, DI), F32),
            jax.ShapeDtypeStruct((KEYS // 4, DI), F32),
        ),
        in_specs=[smem] + [hbm] * 5,
        out_specs=(hbm, hbm),
        scratch_shapes=scratch,
        compiler_params=pltpu.CompilerParams(
            collective_id=0, has_side_effects=True, vmem_limit_bytes=63 * 1024 * 1024
        ),
    )(
        positions,
        queries.reshape(rows, queries.shape[2]),
        latents.T,
        index_queries.reshape(Q * JL, DI),
        index_keys,
        index_weights.T,
    )
    grad_queries, grad_keys = pl.pallas_call(
        deliver,
        out_shape=(
            jax.ShapeDtypeStruct((Q * JL, DI), F32),
            jax.ShapeDtypeStruct((KEYS // 4, DI), F32),
        ),
        in_specs=[hbm, hbm],
        out_specs=(hbm, hbm),
        scratch_shapes=[v((Q * JL, DI), F32), v((KEYS // 4, DI), F32), dma((5,)), dma((5,))],
        compiler_params=pltpu.CompilerParams(vmem_limit_bytes=63 * 1024 * 1024),
    )(grad_queries, grad_keys)
    return grad_queries.reshape(Q, JL, DI), grad_keys


def solution(mesh):
    placed = (
        P(None, "heads", None),
        P("ctx", None),
        P(None, "heads", None),
        P("ctx", None),
        P(None, "heads"),
        P(),
    )
    return jax.shard_map(
        body,
        mesh=mesh,
        in_specs=placed,
        out_specs=(P(None, "heads", None), P(("ctx", "heads"), None)),
        check_vma=False,
    )
```

```python
import functools

import jax
import jax.numpy as jnp
from jax import lax
from jax.experimental import pallas as pl
from jax.experimental.pallas import tpu as pltpu
from jax.sharding import PartitionSpec as P

MESH = pl.DeviceIdType.MESH
F32 = jnp.float32
BF16 = jnp.bfloat16

Q, H, HI, DI = 64, 128, 64, 128
NZ = 8
NG = 8
HL = 32
JL = 16
KEYS = 1024
QB = 8
NB = Q // QB
CH = 32
LOG2E = 1.4426950408889634
SCORE_SCALE = (192 ** (-0.5)) * LOG2E
INDEX_SCALE = (HI * DI) ** (-0.5)
FILL = -1e30
LOSS_SCALE = 1024.0


def kernel(
    pos_ref, q_hbm, lat_hbm, iq_hbm, ik_hbm, wt_hbm,
    gq_ref, gk_ref,
    q_ref, lat_ref, iq_ref, ik_ref, wt_ref,
    prod_a, prod_b, mb, ex, iqf, iqp, iqt, ikt, dots, wpad, w_ref, coef,
    lg, lg_rc, lg_ry, lg_fin,
    tg, tg_rc, tg_ry, tg_co, tg_fin,
    st, st_rz, st2, st_rx, ix, ix_rz, ix2, ix_rx, fac,
    gq_tmp, gq, gq_rx, gz, gz_rx,
    gk_p, gk_rc, gk_s, gk_ry, gsum, gk_out,
    load_sem, pair_send, pair_recv, send_z, recv_z, send_x, recv_x,
):
    c = lax.axis_index("ctx")
    h = lax.axis_index("heads")
    z, g = c % NZ, c // NZ
    core, ylo = h % 2, h // 2
    core_peer = (c, ylo * 2 + (1 - core))
    ylo_peer = (c, (1 - ylo) * 2 + core)
    cross_peer = (c, (1 - ylo) * 2 + (1 - core))
    far = (4, 3, 5, 2, 6, 1, 7)
    z_ids = [(z + k) % NZ for k in far]
    g_ids = [(g + k) % NG for k in far]
    z_peers = [(g * NZ + i, h) for i in z_ids]
    g_peers = [(i * NZ + z, h) for i in g_ids]
    peers = z_peers + g_peers + [core_peer, ylo_peer, cross_peer]

    barrier = pltpu.get_barrier_semaphore()
    for p in peers:
        pl.semaphore_signal(barrier, inc=1, device_id=p, device_id_type=MESH)

    def load(k, src, dst):
        copy = pltpu.make_async_copy(src, dst, load_sem.at[k])
        copy.start()
        return copy

    first_rows, last_rows = pl.ds(0, CH * HL), pl.ds(CH * HL, CH * HL)
    l_iq = load(0, iq_hbm, iq_ref)
    l_ik = load(1, ik_hbm, ik_ref)
    l_wt = load(2, wt_hbm, wt_ref)
    l_lat = load(3, lat_hbm, lat_ref)
    l_q0 = load(4, q_hbm.at[first_rows], q_ref.at[first_rows])
    l_q1 = load(5, q_hbm.at[last_rows], q_ref.at[last_rows])

    def remote(src, dst, send, recv, peer):
        return pltpu.make_async_remote_copy(
            src_ref=src, dst_ref=dst, send_sem=send, recv_sem=recv,
            device_id=peer, device_id_type=MESH,
        )

    def pair(slot, src, dst, peer):
        copy = remote(src, dst, pair_send.at[slot], pair_recv.at[slot], peer)
        copy.start()
        return copy

    def spread(slot, sends, recvs, targets, src, dst):
        copies = [
            remote(src(k), dst(k), sends.at[slot, k], recvs.at[slot, k], p)
            for k, p in enumerate(targets)
        ]
        for copy in copies:
            copy.start()
        return copies

    def wait(copies):
        for copy in copies:
            copy.wait()

    lane = lax.broadcasted_iota(jnp.int32, (QB, 128), 1)
    sub = lax.broadcasted_iota(jnp.int32, (QB, 128), 0)
    key_pos = c * KEYS + lane
    row_iota = lax.broadcasted_iota(jnp.int32, (QB, 1), 0)
    GROUPS = KEYS // 128

    def lanes(n):
        return slice(n * 128, (n + 1) * 128)

    def aligned(start, size, by=None):
        return pl.ds(pl.multiple_of(start, by or size), size)

    def tree(op, parts):
        parts = list(parts)
        while len(parts) > 1:
            parts = [op(*parts[i : i + 2]) if i + 1 < len(parts) else parts[i] for i in range(0, len(parts), 2)]
        return parts[0]

    l_iq.wait()
    iqf[...] = iq_ref[...].astype(F32)

    def permute(b, _):
        for j in range(0, JL, 2):
            two = [iqf[pl.ds(b * 128 + j + i, QB, stride=JL), :] for i in range(2)]
            iqp[aligned(b * 128 + j * QB, 2 * QB), :] = jnp.concatenate(two, axis=0).astype(BF16)
        return 0

    lax.fori_loop(0, NB, permute, 0)
    iqt[...] = iqp[...].T
    l_ik.wait()
    ikt[...] = ik_ref[...].T
    l_wt.wait()
    wpad[...] = jnp.zeros_like(wpad)
    wpad[0:JL, 0:Q] = wt_ref[...] * INDEX_SCALE
    w_ref[...] = wpad[...].T

    for n in range(KEYS // 256):
        at = slice(n * 256, (n + 1) * 256)
        dots[:, at] = jnp.dot(iqp[...], ikt[:, at], preferred_element_type=F32)

    def index_block(b, _):
        wb = w_ref[aligned(b * QB, QB), :]
        ws = [jnp.broadcast_to(wb[:, j : j + 1], (QB, 128)) for j in range(JL)]
        col = jnp.zeros((QB, 1), jnp.int32)
        for i in range(QB):
            col = jnp.where(row_iota == i, pos_ref[b * QB + i], col)
        col = jnp.broadcast_to(col, (QB, 128))
        for n in range(GROUPS):
            total = tree(jnp.add, [
                ws[j] * jnp.maximum(dots[aligned(b * 128 + j * QB, QB), lanes(n)], 0.0)
                for j in range(JL)
            ])
            lg[aligned(b * QB, QB), lanes(n)] = jnp.where(key_pos + n * 128 <= col, total, FILL)
        return 0

    lax.fori_loop(0, NB, index_block, 0, unroll=True)

    def multiply(b, prod):
        rows = aligned(b * (QB * HL), QB * HL)
        for n in range(KEYS // 256):
            at = slice(n * 256, (n + 1) * 256)
            prod[:, at] = jnp.dot(q_ref[rows, :], lat_ref[:, at], preferred_element_type=F32)

    def softmax(b, prod, carry):
        local = b % (CH // QB) * QB

        def peaks(k, ms):
            pos = pos_ref[b * QB + k]
            vis = [key_pos + n * 128 <= pos for n in range(GROUPS)]
            for i in range(HL // QB):
                rows = aligned(k * HL + i * QB, QB)
                m = tree(jnp.maximum, [
                    jnp.where(vis[n], prod[rows, lanes(n)], FILL) for n in range(GROUPS)
                ])
                m = jnp.broadcast_to(jnp.max(m, axis=1, keepdims=True) * SCORE_SCALE, (QB, 128))
                mb[rows, :] = m
                ms = jnp.where(lane == i * 32 + local + k, m, ms)
            return ms

        def masses(k, ls):
            pos = pos_ref[b * QB + k]
            vis = [key_pos + n * 128 <= pos for n in range(GROUPS)]
            for i in range(HL // QB):
                rows = aligned(k * HL + i * QB, QB)
                m = mb[rows, :]
                to = aligned(b * (QB * HL) + k * HL + i * QB, QB)
                es = []
                for n in range(GROUPS):
                    e = jnp.exp2(prod[rows, lanes(n)] * SCORE_SCALE - m)
                    e = jnp.where(vis[n], e, 0.0)
                    ex[to, lanes(n)] = e
                    es.append(e)
                l = jnp.sum(tree(jnp.add, es), axis=1, keepdims=True)
                ls = jnp.where(lane == i * 32 + local + k, l, ls)
            return ls

        ms = lax.fori_loop(0, QB, peaks, carry[0], unroll=True)
        ls = lax.fori_loop(0, QB, masses, carry[1], unroll=True)
        return ms, ls

    def two_blocks(i, carry):
        multiply(2 * i + 1, prod_b)
        carry = softmax(2 * i, prod_a, carry)
        multiply(jnp.minimum(2 * i + 2, NB - 1), prod_a)
        return softmax(2 * i + 1, prod_b, carry)

    def attention(first, last, carry):
        return lax.fori_loop(first, last, two_blocks, carry)

    zero = jnp.zeros((QB, 128), F32)
    half = aligned(core * 32, 32)
    other = aligned((1 - core) * 32, 32)

    l_lat.wait()
    l_q0.wait()
    multiply(0, prod_a)
    l_q1.wait()
    ms, ls = attention(0, 2, (zero, zero))
    st[0, 0:8, :] = ms
    st[0, 8:16, :] = ls
    pl.semaphore_wait(barrier, len(peers))
    s_z0 = spread(0, send_z, recv_z, z_peers, lambda k: st.at[0], lambda k: st_rz.at[0, k])
    lg1 = pair(0, lg.at[other], lg_rc, core_peer)
    carry = attention(2, 3, (zero, zero))
    lg1.wait()
    lg[half, :] = lg[half, :] + lg_rc[...]
    lg2 = pair(1, lg.at[half], lg_ry, ylo_peer)
    ms, ls = attention(3, 4, carry)
    st[1, 0:8, :] = ms
    st[1, 8:16, :] = ls
    s_z1 = spread(1, send_z, recv_z, z_peers, lambda k: st.at[1], lambda k: st_rz.at[1, k])

    def index_stats(b, so_far):
        rows = aligned(b * QB, QB)
        xs = [lg_fin[rows, lanes(n)] * LOG2E for n in range(GROUPS)]
        m = jnp.max(tree(jnp.maximum, xs), axis=1, keepdims=True)
        mm = jnp.broadcast_to(m, (QB, 128))
        l = jnp.sum(tree(jnp.add, [jnp.exp2(x - mm) for x in xs]), axis=1, keepdims=True)
        return jnp.where(lane == b, m, jnp.where(lane == b + 64, l, so_far))

    def combine(own, received):
        parts = [own[...]] + [received[k] for k in range(7)]
        top = tree(jnp.maximum, [p[0:8] for p in parts])
        mass = tree(jnp.add, [p[8:16] * jnp.exp2(p[0:8] - top) for p in parts])
        return top, mass

    def combine_index(own, received):
        parts = [own[...]] + [received[k] for k in range(7)]
        peak = tree(jnp.maximum, parts)
        low = lane < 64
        mass = tree(jnp.add, [
            p * pltpu.roll(jnp.exp2(jnp.where(low, p - peak, 0.0)), 64, 1) for p in parts
        ])
        return jnp.where(low, peak, mass)

    def combined_z(t):
        top, mass = combine(st.at[t], st_rz.at[t])
        st2[t, 0:8, :] = top
        st2[t, 8:16, :] = mass
        return spread(t, send_x, recv_x, g_peers, lambda k: st2.at[t], lambda k: st_rx.at[t, k])

    def factors(t):
        top, mass = combine(st2.at[t], st_rx.at[t])
        fac[t] = jnp.exp2(st[t, 0:8, :] - top) / mass

    def turn(x, shift):
        return pltpu.roll(x, shift % QB, 0)

    def gathered(r):
        r = [r[i] for i in (3, 2, 1, 0, 7, 6, 5, 4)]
        low = sub < 4
        a = [
            jnp.where(low, r[i], r[i + 4]) + turn(jnp.where(low, r[i + 4], r[i]), 4)
            for i in range(4)
        ]
        low = sub % 4 < 2
        b = [jnp.where(low, a[i + 2] + turn(a[i + 2], -2), a[i] + turn(a[i], 2)) for i in range(2)]
        return jnp.where(sub % 2 < 1, b[1] + turn(b[1], -1), b[0] + turn(b[0], 1))

    def target(t):
        f = fac[t]
        for b in range(CH // QB):
            fs = [
                [
                    jnp.broadcast_to(f[:, i * 32 + b * QB + k : i * 32 + b * QB + k + 1], (QB, 128))
                    for i in range(4)
                ]
                for k in range(QB)
            ]
            for n in range(GROUPS):
                r = []
                for k in range(QB):
                    at = (t * (CH // QB) + b) * (QB * HL) + k * HL
                    r.append(tree(jnp.add, [
                        ex[at + i * QB : at + (i + 1) * QB, lanes(n)] * fs[k][i] for i in range(4)
                    ]))
                tg[t, b * QB : (b + 1) * QB, lanes(n)] = gathered(r)

    part = aligned(core * 16, 16)
    other_part = aligned((1 - core) * 16, 16)

    def core_one(t):
        return pair(3 + t, tg.at[t, other_part], tg_rc.at[t], core_peer)

    def across(t):
        tg[t, part, :] = tg[t, part, :] + tg_rc[t]
        mine = tg.at[t, part]
        return [
            pair(5 + t, mine, tg_ry.at[t, part], ylo_peer),
            pair(7 + t, mine, tg_ry.at[t, part], cross_peer),
            pair(11 + t, mine, tg_co.at[t], core_peer),
        ]

    def complete(t, copies):
        wait(copies)
        tg_fin[t, part, :] = tg[t, part, :] + tg_ry[t, part, :]
        tg_fin[t, other_part, :] = tg_co[t] + tg_ry[t, other_part, :]

    def grads(t):
        totals = fac[2]
        for i in range(CH // QB):
            b = t * (CH // QB) + i
            rows = slice(b * QB, (b + 1) * QB)
            peak = jnp.broadcast_to(totals[:, b : b + 1], (QB, 128))
            share = jnp.broadcast_to(LOSS_SCALE / totals[:, b + 64 : b + 65], (QB, 128))
            wb = w_ref[rows, :]
            ws = [jnp.broadcast_to(wb[:, j : j + 1], (QB, 128)) for j in range(JL)]
            for n in range(GROUPS):
                probs = jnp.exp2(lg_fin[rows, lanes(n)] * LOG2E - peak) * share
                grad = probs - tg_fin[t, i * QB : (i + 1) * QB, lanes(n)] * (LOSS_SCALE / H)
                for j in range(0, JL, 2):
                    two = []
                    for jj in (j, j + 1):
                        d = dots[b * 128 + jj * QB : b * 128 + (jj + 1) * QB, lanes(n)]
                        two.append(jnp.where(d > 0.0, grad * ws[jj], 0.0))
                    at = slice(b * 128 + j * QB, b * 128 + (j + 2) * QB)
                    coef[at, lanes(n)] = jnp.concatenate(two, axis=0).astype(BF16)
        gq_tmp[...] = jnp.dot(
            coef[t * 512 : (t + 1) * 512, :], ik_ref[...], preferred_element_type=F32
        )
        for i in range(CH // QB):
            for k in range(QB):
                gq[t, i * 128 + k * JL : i * 128 + (k + 1) * JL, :] = gq_tmp[
                    pl.ds(i * 128 + k, JL, stride=QB), :
                ]
        return spread(
            2 + t, send_x, recv_x, g_peers,
            lambda k: gq.at[t, aligned(g_ids[k] * 64, 64)], lambda k: gq_rx.at[t, k],
        )

    def sum_x(t):
        mine = gq[t, aligned(g * 64, 64), :]
        gz[t] = tree(jnp.add, [mine] + [gq_rx[t, k] for k in range(7)])
        gz_rx[t, z] = gz[t]
        return spread(
            2 + t, send_z, recv_z, z_peers, lambda k: gz.at[t], lambda k: gz_rx.at[t, z]
        )

    def sum_z(t):
        mine = aligned(t * 512 + g * 64, 64)
        gsum[t] = tree(jnp.add, [gz_rx[t, k] for k in range(NZ)])
        copies = spread(
            4 + t, send_x, recv_x, g_peers, lambda k: gsum.at[t], lambda k: gq_ref.at[mine]
        )
        return copies + [load(t, gsum.at[t], gq_ref.at[mine])]

    lg2.wait()
    lg_fin[half, :] = lg[half, :] + lg_ry[...]
    lg3 = pair(2, lg_fin.at[half], lg_fin.at[half], core_peer)
    wait(s_z0)
    s_x0 = combined_z(0)
    lg3.wait()
    ix[...] = lax.fori_loop(0, NB, index_stats, zero, unroll=True)
    i_z = spread(4, send_z, recv_z, z_peers, lambda k: ix, lambda k: ix_rz.at[k])
    wait(s_z1)
    s_x1 = combined_z(1)
    wait(s_x0)
    factors(0)
    target(0)
    one0 = core_one(0)
    wait(i_z)
    ix2[...] = combine_index(ix, ix_rz)
    i_x = spread(6, send_x, recv_x, g_peers, lambda k: ix2, lambda k: ix_rx.at[k])
    one0.wait()
    across0 = across(0)
    wait(s_x1)
    factors(1)
    target(1)
    one1 = core_one(1)
    one1.wait()
    across1 = across(1)
    complete(0, across0)
    wait(i_x)
    fac[2] = combine_index(ix2, ix_rx)
    rs0 = grads(0)
    complete(1, across1)
    rs1 = grads(1)

    for piece in range(4):
        gk_p[piece % 2, piece // 2] = jnp.dot(
            iqt[...], coef[:, piece * 256 : (piece + 1) * 256], preferred_element_type=F32
        )
    gk1 = pair(9, gk_p.at[1 - core], gk_rc, core_peer)
    wait(rs0)
    sz0 = sum_x(0)
    gk1.wait()
    gk_s[...] = gk_p[core] + gk_rc[...]
    gk2 = pair(10, gk_s.at[1 - ylo], gk_ry, ylo_peer)
    wait(rs1)
    sz1 = sum_x(1)
    gk2.wait()
    gk_out[...] = (gk_s[ylo] + gk_ry[...]).T
    gk_store = load(2, gk_out, gk_ref)
    wait(sz0)
    ag0 = sum_z(0)
    wait(sz1)
    ag1 = sum_z(1)
    wait(ag0)
    wait(ag1)
    gk_store.wait()


def deliver(gq_in, gk_in, gq_out, gk_out, gq_buf, gk_buf, arrive, leave):
    part = Q * JL // 4

    def piece(k):
        return pl.ds(k * part, part)

    first = [pltpu.make_async_copy(gk_in, gk_buf, arrive.at[4])]
    last = [pltpu.make_async_copy(gk_buf, gk_out, leave.at[4])]
    for k in range(4):
        first.append(pltpu.make_async_copy(gq_in.at[piece(k)], gq_buf.at[piece(k)], arrive.at[k]))
        last.append(pltpu.make_async_copy(gq_buf.at[piece(k)], gq_out.at[piece(k)], leave.at[k]))
    for copy in first:
        copy.start()
    for one, two in zip(first, last):
        one.wait()
        two.start()
    for copy in last:
        copy.wait()


def body(queries, latents, index_queries, index_keys, index_weights, positions):
    hbm = pl.BlockSpec(memory_space=pltpu.HBM)
    smem = pl.BlockSpec(memory_space=pltpu.SMEM)
    rows = Q * HL
    v = pltpu.VMEM
    dma = pltpu.SemaphoreType.DMA
    scratch = [
        v((rows, queries.shape[2]), BF16),
        v((queries.shape[2], KEYS), BF16),
        v((Q * JL, DI), BF16),
        v((KEYS, DI), BF16),
        v((JL, Q), F32),
        v((QB * HL, KEYS), F32),
        v((QB * HL, KEYS), F32),
        v((QB * HL, 128), F32),
        v((rows, KEYS), F32),
        v((Q * JL, DI), F32),
        v((Q * JL, DI), BF16),
        v((DI, Q * JL), BF16),
        v((DI, KEYS), BF16),
        v((Q * JL, KEYS), F32),
        v((128, 128), F32),
        v((128, 128), F32),
        v((Q * JL, KEYS), BF16),
        v((Q, KEYS), F32), v((32, KEYS), F32), v((32, KEYS), F32), v((Q, KEYS), F32),
        v((2, CH, KEYS), F32), v((2, 16, KEYS), F32), v((2, CH, KEYS), F32),
        v((2, 16, KEYS), F32), v((2, CH, KEYS), F32),
        v((2, 16, 128), F32), v((2, 7, 16, 128), F32),
        v((2, 16, 128), F32), v((2, 7, 16, 128), F32),
        v((8, 128), F32), v((7, 8, 128), F32), v((8, 128), F32), v((7, 8, 128), F32),
        v((3, 8, 128), F32),
        v((512, DI), F32), v((2, 512, DI), F32), v((2, 7, 64, DI), F32),
        v((2, 64, DI), F32), v((2, NZ, 64, DI), F32),
        v((2, 2, DI, 256), F32), v((2, DI, 256), F32), v((2, DI, 256), F32), v((DI, 256), F32),
        v((2, 64, DI), F32), v((KEYS // 4, DI), F32),
        dma((6,)), dma((13,)), dma((13,)), dma((5, 7)), dma((5, 7)), dma((7, 7)), dma((7, 7)),
    ]
    grad_queries, grad_keys = pl.pallas_call(
        kernel,
        out_shape=(
            jax.ShapeDtypeStruct((Q * JL, DI), F32),
            jax.ShapeDtypeStruct((KEYS // 4, DI), F32),
        ),
        in_specs=[smem] + [hbm] * 5,
        out_specs=(hbm, hbm),
        scratch_shapes=scratch,
        compiler_params=pltpu.CompilerParams(
            collective_id=0, has_side_effects=True, vmem_limit_bytes=63 * 1024 * 1024
        ),
    )(
        positions,
        queries.reshape(rows, queries.shape[2]),
        latents.T,
        index_queries.reshape(Q * JL, DI),
        index_keys,
        index_weights.T,
    )
    grad_queries, grad_keys = pl.pallas_call(
        deliver,
        out_shape=(
            jax.ShapeDtypeStruct((Q * JL, DI), F32),
            jax.ShapeDtypeStruct((KEYS // 4, DI), F32),
        ),
        in_specs=[hbm, hbm],
        out_specs=(hbm, hbm),
        scratch_shapes=[v((Q * JL, DI), F32), v((KEYS // 4, DI), F32), dma((5,)), dma((5,))],
        compiler_params=pltpu.CompilerParams(vmem_limit_bytes=63 * 1024 * 1024),
    )(grad_queries, grad_keys)
    return grad_queries.reshape(Q, JL, DI), grad_keys


def solution(mesh):
    placed = (
        P(None, "heads", None),
        P("ctx", None),
        P(None, "heads", None),
        P("ctx", None),
        P(None, "heads"),
        P(),
    )
    return jax.shard_map(
        body,
        mesh=mesh,
        in_specs=placed,
        out_specs=(P(None, "heads", None), P(("ctx", "heads"), None)),
        check_vma=False,
    )
```
